32 devices in a mesh: sec: 4 (over x, core), dev: 8 (over z, y).
Axes of the slice: x: 2, y: 2, z: 4, core: 2. Of those that a mesh axis runs over, the one named last changes fastest.
Arguments:
- tokens: bfloat16 [256, 7168], P('dev', 'sec'), may hold values from -6 to 6
- routes: int32 [256, 8], P('dev'), may hold values from 0 to 23, all different within a row; in each aligned block of 32 rows (0 to 31, 32 to 63, ...) at most 16 rows name the same one
- scores: float32 [256, 8], P('dev'), may hold values from 0.25 to 1
- gate_up_codes: int32 [32, 2, 2, 896, 1024], P(('sec', 'dev')), may hold values from 0 to 255, as said below
- down_codes: int32 [32, 2, 128, 7168], P(('sec', 'dev')), may hold values from 0 to 255, as said below
- model_signs: int32 [32, 2, 7168], P(('sec', 'dev')), may hold values from 0 to 1, as said below
- hidden_signs: int32 [32, 1024], P(('sec', 'dev')), may hold values from 0 to 1, as said below
- gate_up_books: bfloat16 [2, 2, 256, 8], replicated, may hold values from -0.046875 to 0.046875
- down_books: bfloat16 [2, 256, 8], replicated, may hold values from -0.125 to 0.125
Outputs:
- mixed: bfloat16 [256, 7168], P('dev', 'sec')
The draws below stay inside these ranges and needn't reach their ends.
Inputs may be any that keep to these rules, and one draw needn't show every extreme that they name: `gate_up_codes`: stacked experts 0 to 7 are equal copies of the shared expert; stacked expert 8 + e is routed expert e. `down_codes`: stacked as in gate_up_codes. `model_signs`: stacked as in gate_up_codes. `hidden_signs`: stacked as in gate_up_codes. `routes`: each token names 8 different routed experts; within each aligned block of 32 tokens no expert is named by more than 16 tokens.
All inputs are finite; a program needn't handle non-finite values.
Results may differ from the reference program's by a relative error of at most 0.0096.
Values may be sent and summed in bfloat16 or wider, within the bound.
No kernel may reach another device: no remote copies, remote signals or barrier semaphores. Data moves between devices by JAX's collectives and lax.ppermute only.
A program may use at most 192 MiB of HBM per device.

```python
import math
import jax
import jax.numpy as jnp
import numpy as np
from jax import lax

D = 7168
HID = 1024
HAD = 128
GROUP = 8
KBOOK = 256
TOPK = 8
TOK_DEV = 32
TOKENS = 256
EXPERTS = 24
CAP = 16
SLOTS = 128
N_DEV = 8


def stacked_integers(key, shape, highest):
    shared = jax.random.randint(jax.random.fold_in(key, 1), (1,) + shape, 0, highest, dtype=jnp.int32)
    routed = jax.random.randint(jax.random.fold_in(key, 2), (EXPERTS,) + shape, 0, highest, dtype=jnp.int32)
    return jnp.concatenate([jnp.broadcast_to(shared, (N_DEV,) + shape), routed], 0).astype(jnp.int32)


def draw_gate_up_codes(key, part):
    return stacked_integers(jax.random.fold_in(key, 101), (2, 2, D // GROUP, HID), KBOOK)


def draw_down_codes(key, part):
    return stacked_integers(jax.random.fold_in(key, 202), (2, HID // GROUP, D), KBOOK)


def draw_model_signs(key, part):
    return stacked_integers(jax.random.fold_in(key, 303), (2, D), 2)


def draw_hidden_signs(key, part):
    return stacked_integers(jax.random.fold_in(key, 404), (HID,), 2)


def block_levels(stream_key, extent, shards, least, largest):
    gain, own = 1.0, jax.random.fold_in(stream_key, 6)
    for axis_at, parts in shards:
        draws = jnp.exp(jax.random.uniform(jax.random.fold_in(own, axis_at), (parts,), jnp.float32, least / len(shards), largest / len(shards)))
        gain = gain * jnp.repeat(draws, extent[axis_at] // parts).reshape([-1 if axis == axis_at else 1 for axis in range(len(extent))])
    return gain


def routed_block(key, own, number, rows, count, top, reach, slope):
    ranking = jax.random.permutation(key, count)
    heavy_load, common = portions_of(count, rows * top, reach, slope, True), portions_of(count, rows * top, reach, slope, False)
    places = jnp.arange(count)

    def named(tallies, offset_by):
        used = int((tallies > 0).sum())
        fixed = max(1, used // 4)
        shifted = fixed + (places - fixed + offset_by * (used - fixed)) % max(1, count - fixed)
        return jnp.zeros((count,), jnp.int32).at[ranking[jnp.where(places < fixed, places, shifted)]].set(jnp.asarray(tallies, jnp.int32))

    tallies = jnp.where(number % 4 == 0, named(heavy_load, number // 4), named(common, number - number // 4 - 1))
    mixed = jax.random.permutation(jax.random.fold_in(own, 3), count)
    giver, taker = mixed[0:count // 2 * 2:2], mixed[1:count // 2 * 2:2]
    margin = jnp.minimum(tallies[giver] - 1, reach - tallies[taker]) // 2
    margin = jnp.where((giver == ranking[0]) | (taker == ranking[0]) | (tallies[taker] == 0), 0, jnp.maximum(margin, 0))
    shifted = jax.random.randint(jax.random.fold_in(own, 4), (count // 2,), 0, 1 << 20) % (margin + 1)
    tallies = tallies.at[giver].add(-shifted).at[taker].add(shifted)
    members = jnp.searchsorted(jnp.cumsum(tallies), jnp.arange(rows * top), side="right").astype(jnp.int32)
    listing = members.reshape(top, rows).T
    listing = listing[jax.random.permutation(jax.random.fold_in(own, 1), rows)]
    offset_by = jax.random.randint(jax.random.fold_in(own, 2), (rows, 1), 0, top)
    return jnp.take_along_axis(listing, (jnp.arange(top)[None, :] + offset_by) % top, axis=1)


def portions_of(number_of, total, most, skew, full):
    portions = [(1 << 20) // math.isqrt(standing ** skew) + 1 for standing in range(1, number_of + 1)]
    largest = most if full else min(most, max(-(-total // number_of), total * portions[0] // sum(portions)))
    least = 1 if total - largest >= number_of - 1 else 0
    holding, surplus = [largest] + [least] * (number_of - 1), total - largest - least * (number_of - 1)
    while surplus > 0:
        free = [i for i in range(1, number_of) if holding[i] < largest] or [i for i in range(1, number_of) if holding[i] < most]
        mass, budget = sum([portions[i] for i in free]), surplus
        for i in free:
            extra = min(most - holding[i], max(1, budget * portions[i] // mass), surplus)
            holding[i] = holding[i] + extra
            surplus = surplus - extra
    return np.array(holding)


def gaussian(key, extent, width, limit, cuts=(), held_as=jnp.bfloat16):
    drawn = jax.random.normal(key, extent, jnp.float32) * width
    if len(cuts) > 0:
        drawn = block_levels(key, extent, cuts, -0.22, 0.18) * drawn
    return jnp.clip(drawn, min=-limit, max=limit).astype(held_as)


def setup_inputs(seed: int = 0) -> dict:
    arg_keys = jax.random.split(jax.random.key(seed), 10)
    tokens = gaussian(arg_keys[0], (TOKENS, D), 1.0, 6.0, ((0, 8), (1, 4)))
    routes_keys = jax.random.split(jax.random.fold_in(arg_keys[1], 1), TOKENS // TOK_DEV)
    routes_turns = jax.random.permutation(jax.random.fold_in(arg_keys[1], 3), TOKENS // TOK_DEV)
    routes = jax.vmap(lambda own, number: routed_block(jax.random.fold_in(arg_keys[1], 2), own, number, TOK_DEV, EXPERTS, TOPK, CAP, 2))(routes_keys, routes_turns).reshape((TOKENS, TOPK))
    scores = jnp.clip(jnp.exp(math.log(1.0) - 1.3862944 * jax.random.uniform(arg_keys[2], (TOKENS, TOPK), jnp.float32) ** block_levels(arg_keys[2], (TOKENS, TOPK), ((0, 8),), -0.2, 0.2)), 0.25, 1.0)
    gate_up_codes = draw_gate_up_codes(jax.random.fold_in(arg_keys[9], 71), 0)
    down_codes = draw_down_codes(jax.random.fold_in(arg_keys[9], 71), 0)
    model_signs = draw_model_signs(jax.random.fold_in(arg_keys[9], 71), 0)
    hidden_signs = draw_hidden_signs(jax.random.fold_in(arg_keys[9], 71), 0)
    gate_up_books = gaussian(arg_keys[7], (2, 2, KBOOK, GROUP), (2 * D) ** -0.5, 0.046875)
    down_books = gaussian(arg_keys[8], (2, KBOOK, GROUP), (2 * HID) ** -0.5, 0.125)
    return dict(tokens=tokens, routes=routes, scores=scores, gate_up_codes=gate_up_codes, down_codes=down_codes, model_signs=model_signs, hidden_signs=hidden_signs, gate_up_books=gate_up_books, down_books=down_books)


def hadamard_table(length):
    sylvester = np.ones((1, 1), np.float32)
    while sylvester.shape[0] < length:
        sylvester = np.concatenate([np.concatenate([sylvester, sylvester], 1), np.concatenate([sylvester, -sylvester], 1)], 0)
    return sylvester

def rotate_exact(values):
    row_count, row_width = values.shape
    sylvester = jnp.asarray(hadamard_table(HAD), jnp.float32)
    blocks = values.astype(jnp.float32).reshape(row_count, row_width // HAD, HAD)
    turned = jnp.einsum('rbi,ij->rbj', blocks, sylvester, precision=lax.Precision.HIGHEST)
    return (turned * (1.0 / math.sqrt(HAD))).reshape(row_count, row_width)

def decode_pair(code_words, codebooks):
    matrices = []
    for which in range(2):
        first = codebooks[which, 0].astype(jnp.float32)[code_words[which, 0]]
        second = codebooks[which, 1].astype(jnp.float32)[code_words[which, 1]]
        summed = (first + second).transpose(0, 2, 1)
        matrices.append(summed.reshape(summed.shape[0] * summed.shape[1], summed.shape[2]).astype(jnp.bfloat16))
    return jnp.stack(matrices, 0)

def decode_down(code_words, codebooks):
    first = codebooks[0].astype(jnp.float32)[code_words[0]]
    second = codebooks[1].astype(jnp.float32)[code_words[1]]
    summed = (first + second).transpose(0, 2, 1)
    return summed.reshape(summed.shape[0] * summed.shape[1], summed.shape[2]).astype(jnp.bfloat16)

def matmul(left, right):
    return jnp.dot(left.astype(jnp.float32), right.astype(jnp.float32), precision=lax.Precision.HIGHEST)

def expert_apply(row_block, weights_in, weights_down, sign_model, sign_hidden):
    front_sign = (2 * sign_model[0] - 1).astype(jnp.bfloat16)
    back_sign = (2 * sign_model[1] - 1).astype(jnp.float32)
    middle_sign = (2 * sign_hidden - 1).astype(jnp.bfloat16)
    turned = rotate_exact(row_block * front_sign).astype(jnp.bfloat16)
    gate_part = matmul(turned, weights_in[0])
    up_part = matmul(turned, weights_in[1])
    hidden = (jax.nn.silu(gate_part) * up_part).astype(jnp.bfloat16)
    folded = rotate_exact(hidden * middle_sign).astype(jnp.bfloat16)
    outcome = matmul(folded, weights_down)
    return (back_sign * rotate_exact(outcome)).astype(jnp.bfloat16)

def reference(tokens, routes, scores, gate_up_codes, down_codes, model_signs, hidden_signs, gate_up_books, down_books):
    gates = (2.5 * scores / lax.optimization_barrier(jnp.sum(scores, axis=1, keepdims=True))).astype(jnp.bfloat16)
    hits = (routes[:, :, None] == jnp.arange(EXPERTS, dtype=jnp.int32)).astype(jnp.int32)
    counted = lax.optimization_barrier(jnp.sum(hits, axis=1)).reshape(N_DEV, TOK_DEV, EXPERTS)
    before = (jnp.cumsum(counted, axis=1) - counted).reshape(TOKENS, EXPERTS)
    slots = lax.optimization_barrier(jnp.sum(hits * before[:, None, :], axis=2)).astype(jnp.int32)
    source = (jnp.arange(TOKENS, dtype=jnp.int32) // TOK_DEV)[:, None]
    slot_row = (source * CAP + slots).astype(jnp.int32)
    token_ids = jnp.broadcast_to(jnp.arange(TOKENS, dtype=jnp.int32)[:, None], routes.shape)
    owners = jnp.full((EXPERTS, SLOTS), TOKENS, jnp.int32).at[routes, slot_row].set(token_ids)
    padded = jnp.concatenate([tokens, jnp.zeros((1, D), tokens.dtype)], 0)

    def run_expert(per_expert):
        code_pair, code_down, sign_model, sign_hidden, owner_rows = per_expert
        weights_in = decode_pair(code_pair, gate_up_books)
        weights_down = decode_down(code_down, down_books)
        return expert_apply(padded[owner_rows], weights_in, weights_down, sign_model, sign_hidden)
    outputs = lax.map(run_expert, (gate_up_codes[N_DEV:], down_codes[N_DEV:], model_signs[N_DEV:], hidden_signs[N_DEV:], owners))
    shared = expert_apply(tokens, decode_pair(gate_up_codes[0], gate_up_books), decode_down(down_codes[0], down_books), model_signs[0], hidden_signs[0])
    picked = outputs[routes, slot_row].astype(jnp.float32)
    total = shared.astype(jnp.float32) + lax.optimization_barrier(jnp.sum(gates.astype(jnp.float32)[:, :, None] * picked, axis=1))
    return total.astype(jnp.bfloat16)
```

```python
import math

import jax
import jax.numpy as jnp
import numpy as np
from jax import lax
from jax.experimental import pallas as pl
from jax.experimental.pallas import tpu as pltpu
from jax.sharding import PartitionSpec as P

HAD = 128
LANES = 128
ROWS = 16
VMEM = 56 << 20
ROUTED_SCALE = 2.5
UNIT = 1.0 / math.sqrt(HAD)
f32, bf16, i16, i32 = jnp.float32, jnp.bfloat16, jnp.int16, jnp.int32


def hadamard_table(length):
    sylvester = np.ones((1, 1), np.float32)
    while sylvester.shape[0] < length:
        sylvester = np.concatenate(
            [np.concatenate([sylvester, sylvester], 1), np.concatenate([sylvester, -sylvester], 1)],
            0,
        )
    return sylvester


def coded_order(group):
    return np.arange(HAD).reshape(HAD // group, group).T.reshape(-1)


def dot(left, right):
    return jnp.dot(left, right, preferred_element_type=f32)


def lookup(table, index):
    dims = lax.GatherDimensionNumbers(
        offset_dims=(),
        collapsed_slice_dims=(1,),
        start_index_map=(1,),
        operand_batching_dims=(0,),
        start_indices_batching_dims=(0,),
    )
    return lax.gather(
        table, index[..., None], dims, (1, 1), mode=lax.GatherScatterMode.PROMISE_IN_BOUNDS
    )


def book_tables(books):
    lead = books.shape[:-2]
    entries, group = books.shape[-2:]
    halves = entries // LANES
    turned = jnp.swapaxes(books, -1, -2).reshape(lead + (group, halves, 1, LANES))
    return jnp.broadcast_to(turned, lead + (group, halves, ROWS, LANES))


def decode_tile(code_words, table, group):
    sums = [None] * group
    for book in range(2):
        words = code_words(book).astype(i16)
        low = words & (LANES - 1)
        upper = words > LANES - 1
        found = [
            (lookup(table(book, i, 0), low), lookup(table(book, i, 1), low)) for i in range(group)
        ]
        for i in range(group):
            value = jnp.where(upper, found[i][1], found[i][0])
            sums[i] = value if book == 0 else sums[i] + value
    return sums


def decode_in(section, codes, tables, weights, order, place):
    _, mats, books, groups, hidden = codes.shape
    sections = 4
    group = tables.shape[2]
    share = groups // sections
    cols = 256

    def body(section_ref, codes_ref, tables_ref, *rest):
        out = rest[-1]
        for h in range(cols // LANES):
            lanes = slice(h * LANES, (h + 1) * LANES)
            for g in range(share // ROWS):
                tiles = decode_tile(
                    lambda c: codes_ref[0, 0, c, g * ROWS : (g + 1) * ROWS, lanes],
                    lambda c, i, half: tables_ref[0, c, i, half],
                    group,
                )
                for i in range(group):
                    at = (g * group + i) * ROWS
                    out[0, at : at + ROWS, lanes] = tiles[i]

    in_specs = [
        pl.BlockSpec(
            (1, 1, books, share, cols), lambda m, h, s: (0, m, 0, jnp.bitwise_xor(s[0], order), h)
        ),
        pl.BlockSpec((1,) + tables.shape[1:], lambda m, h, s: (m, 0, 0, 0, 0, 0)),
    ]
    operands = [section, codes, tables]
    aliases = {}
    if weights is not None:
        in_specs.append(pl.BlockSpec(memory_space=pl.ANY))
        operands.append(weights)
        aliases = {3: 0}
    return pl.pallas_call(
        body,
        grid_spec=pltpu.PrefetchScalarGridSpec(
            num_scalar_prefetch=1,
            grid=(mats, hidden // cols),
            in_specs=in_specs,
            out_specs=pl.BlockSpec((1, share * group, cols), lambda m, h, s: (m, place, h)),
        ),
        out_shape=jax.ShapeDtypeStruct((mats, groups * group, hidden), bf16),
        input_output_aliases=aliases,
        compiler_params=pltpu.CompilerParams(vmem_limit_bytes=VMEM),
        name="decode_in",
    )(*operands)


def rotate(values, table):
    parts = []
    for b in range(values.shape[1] // HAD):
        parts.append((dot(values[:, b * HAD : (b + 1) * HAD], table) * UNIT).astype(bf16))
    return jnp.concatenate(parts, 1)


def project(pick, pieces, weights, front, middle, had):
    slots, token_total = pick.shape
    steps = len(pieces)
    width = pieces[0].shape[1]
    hidden = weights.shape[2]

    def body(*refs):
        pick_ref, *piece_refs = refs[: 1 + steps]
        weights_ref, front_ref, middle_ref, had_ref, out, total, picked = refs[1 + steps :]
        step = pl.program_id(0)
        for at in range(steps):

            @pl.when(step == at)
            def _():
                picked[...] = piece_refs[at][...]

        rows = dot(pick_ref[...], picked[...]).astype(bf16) * front_ref[0]
        turned = rotate(rows, had_ref[...])
        for m in range(2):
            part = dot(turned, weights_ref[m])
            total[m] = jnp.where(step == 0, part, total[m] + part)

        @pl.when(step == steps - 1)
        def _():
            acted = (jax.nn.silu(total[0]) * total[1]).astype(bf16)
            out[...] = rotate(acted * middle_ref[...], had_ref[...])

    whole = lambda shape: pl.BlockSpec(shape, lambda s: (0,) * len(shape))
    return pl.pallas_call(
        body,
        grid=(steps,),
        in_specs=[whole(pick.shape)]
        + [whole(p.shape) for p in pieces]
        + [
            pl.BlockSpec((2, width, hidden), lambda s: (0, s, 0)),
            pl.BlockSpec((1, 1, width), lambda s: (s, 0, 0)),
            whole(middle.shape),
            whole(had.shape),
        ],
        out_specs=whole((slots, hidden)),
        out_shape=jax.ShapeDtypeStruct((slots, hidden), bf16),
        scratch_shapes=[
            pltpu.VMEM((2, slots, hidden), f32),
            pltpu.VMEM((token_total, width), bf16),
        ],
        compiler_params=pltpu.CompilerParams(vmem_limit_bytes=VMEM),
        name="project",
    )(pick, *pieces, weights, front, middle, had)


def produce(section, codes, tables, folded, back, had, spread, order, chunk, chunks):
    _, books, groups, width = codes.shape
    sections = 4
    group = tables.shape[1]
    slots, hidden = folded.shape
    token_total = spread.shape[0]
    steps = width // sections // chunks // LANES
    pair = 2

    def body(section_ref, codes_ref, tables_ref, folded_ref, back_ref, had_ref, spread_ref, out):
        outcome = None
        for p in range(groups // ROWS // pair):
            tiles = []
            for g in range(p * pair, (p + 1) * pair):
                tiles += decode_tile(
                    lambda c: codes_ref[0, c, g * ROWS : (g + 1) * ROWS, :],
                    lambda c, i, half: tables_ref[c, i, half],
                    group,
                )
            depth = pair * group * ROWS
            part = dot(folded_ref[:, p * depth : (p + 1) * depth], jnp.concatenate(tiles, 0))
            outcome = part if outcome is None else outcome + part
        high = outcome.astype(bf16)
        left = outcome - high.astype(f32)
        mid = left.astype(bf16)
        low = (left - mid.astype(f32)).astype(bf16)
        table = had_ref[...]
        turned = (dot(high, table) + (dot(mid, table) + dot(low, table))) * UNIT
        result = (back_ref[...] * turned).astype(bf16)
        out[...] = dot(spread_ref[...], result).astype(bf16)

    def column(j, s):
        return (jnp.bitwise_xor(s[0], order) * chunks + chunk) * steps + j

    whole = lambda shape: pl.BlockSpec(shape, lambda j, s: (0,) * len(shape))
    return pl.pallas_call(
        body,
        grid_spec=pltpu.PrefetchScalarGridSpec(
            num_scalar_prefetch=1,
            grid=(steps,),
            in_specs=[
                pl.BlockSpec((1, books, groups, LANES), lambda j, s: (0, 0, 0, column(j, s))),
                whole(tables.shape),
                whole(folded.shape),
                pl.BlockSpec((1, LANES), lambda j, s: (0, column(j, s))),
                whole(had.shape),
                whole(spread.shape),
            ],
            out_specs=pl.BlockSpec((token_total, LANES), lambda j, s: (0, j)),
        ),
        out_shape=jax.ShapeDtypeStruct((token_total, steps * LANES), bf16),
        compiler_params=pltpu.CompilerParams(vmem_limit_bytes=VMEM),
        name="produce",
    )(section, codes, tables, folded, back, had, spread)


def swap(values, axis, stride):
    size = lax.axis_size(axis)
    return lax.ppermute(values, axis, [(i, i ^ stride) for i in range(size)])


def per_device(
    tokens,
    routes,
    scores,
    gate_up_codes,
    down_codes,
    model_signs,
    hidden_signs,
    gate_up_books,
    down_books,
):
    sections = lax.axis_size("sec")
    devices = lax.axis_size("dev")
    section = lax.axis_index("sec")
    device = lax.axis_index("dev")
    token_count, quarter = tokens.shape
    width = quarter * sections
    token_total = token_count * devices
    slots = 4 * token_count
    group = gate_up_books.shape[-1]
    chunks = 2
    half = quarter // chunks
    strides = [1 << b for b in range(devices.bit_length() - 1)]
    section_word = section.astype(i32).reshape(1)

    relative = [0]
    for stride in reversed(strides):
        relative = relative + [b ^ stride for b in relative]
    places = [0, 2, 1, 3]

    gates = (ROUTED_SCALE * scores / jnp.sum(scores, axis=1, keepdims=True)).astype(bf16)
    facts = jnp.concatenate([routes.astype(f32), gates.astype(f32)], 1)
    facts = lax.all_gather(facts, "dev", axis=0)
    source = jnp.bitwise_xor(jnp.asarray(relative, i32), device.astype(i32))
    facts = jnp.take(facts, source, axis=0).reshape(token_total, -1)
    top = routes.shape[1]
    expert = ((section - 1) * devices + device).astype(f32)
    named = facts[:, :top] == expert
    hit = jnp.any(named, axis=1)
    gate = jnp.sum(jnp.where(named, facts[:, top:], 0.0), axis=1)
    earlier = (jnp.arange(token_total)[:, None] < jnp.arange(token_total)[None, :]).astype(f32)
    slot = jnp.sum(jnp.where(hit[:, None], earlier, 0.0), axis=0)
    slot = jnp.where(hit, slot, -1.0)
    shared = section == 0
    token_id = jnp.arange(token_total)
    own = token_id < token_count
    slot = jnp.where(shared, jnp.where(own, token_id.astype(f32), -1.0), slot)
    gate = jnp.where(shared, 1.0, gate)
    slot_id = jnp.arange(slots).astype(f32)
    pick = (slot_id[:, None] == slot[None, :]).astype(bf16)
    spread = jnp.where(slot[:, None] == slot_id[None, :], gate[:, None], 0.0).astype(bf16)

    tables_in = book_tables(gate_up_books)
    tables_down = book_tables(down_books)
    sylvester = hadamard_table(HAD)
    had_coded = jnp.asarray(sylvester[:, coded_order(group)], bf16)
    had = jnp.asarray(sylvester, bf16)
    front = (2 * model_signs[0, 0] - 1).astype(bf16).reshape(sections, chunks, 1, half)
    front = jnp.take(front, jnp.bitwise_xor(jnp.asarray(places, i32), section.astype(i32)), axis=0)
    front = front.reshape(sections * chunks, 1, half)
    back = (2 * model_signs[0, 1] - 1).astype(f32).reshape(1, width)
    middle = (2 * hidden_signs - 1).astype(bf16)

    def fence(*values):
        return lax.optimization_barrier(values)

    first, second = tokens[:, :half], tokens[:, half:]
    gathered = []
    for part in (first, second):
        gathered.append([part] + [swap(part, "dev", b) for b in relative[1 : devices // 2]])
    weights = decode_in(section_word, gate_up_codes, tables_in, None, places[0], 0)
    weights, gathered = fence(weights, gathered)
    first, second = [jnp.concatenate(g, 0) for g in gathered]
    first_near = swap(first, "dev", 1)
    second_cross = swap(second, "sec", 2)
    weights, first, second = fence(weights, first, second)
    weights = decode_in(section_word, gate_up_codes, tables_in, weights, places[1], 1)
    weights, first_near, second_cross = fence(weights, first_near, second_cross)
    first = jnp.concatenate([first, first_near], 0)
    first_cross = swap(first, "sec", 2)
    second_near = swap(second, "dev", 1)
    second_both = swap(second_cross, "dev", 1)
    weights = decode_in(section_word, gate_up_codes, tables_in, weights, places[2], 2)
    weights, first_cross, second_near, second_both = fence(
        weights, first_cross, second_near, second_both
    )
    second = jnp.concatenate([second, second_near], 0)
    second_cross = jnp.concatenate([second_cross, second_both], 0)
    pieces = [first, second, first_cross, second_cross]
    pieces = pieces + [swap(p, "sec", 1) for p in pieces]
    weights = decode_in(section_word, gate_up_codes, tables_in, weights, places[3], 3)

    folded = project(pick, pieces, weights, front, middle, had_coded)

    made = {}
    for order, chunk in ((3, 0), (2, 0), (3, 1), (2, 1), (1, 0), (0, 0), (1, 1), (0, 1)):
        made[order, chunk] = produce(
            section_word, down_codes, tables_down, folded, back, had, spread, order, chunk, chunks
        )
        folded, made[order, chunk] = fence(folded, made[order, chunk])
    outs = []
    for chunk in range(chunks):
        crossing = made[2, chunk].astype(f32) + swap(made[3, chunk], "sec", 1).astype(f32)
        crossed = swap(crossing.astype(bf16), "sec", 2).astype(f32)
        total = made[0, chunk].astype(f32) + swap(made[1, chunk], "sec", 1).astype(f32) + crossed
        for stride in strides:
            rows = total.shape[0] // 2
            sent = swap(total[rows:].astype(bf16), "dev", stride)
            total = total[:rows] + sent.astype(f32)
        outs.append(total.astype(bf16))
    return jnp.concatenate(outs, 1)


def solution(mesh):
    in_specs = (
        P("dev", "sec"),
        P("dev", None),
        P("dev", None),
        P(("sec", "dev"), None, None, None, None),
        P(("sec", "dev"), None, None, None),
        P(("sec", "dev"), None, None),
        P(("sec", "dev"), None),
        P(),
        P(),
    )
    out_specs = P("dev", "sec")
    return jax.shard_map(
        per_device, mesh=mesh, in_specs=in_specs, out_specs=out_specs, check_vma=False
    )
```

```python
import math

import jax
import jax.numpy as jnp
import numpy as np
from jax import lax
from jax.experimental import pallas as pl
from jax.experimental.pallas import tpu as pltpu
from jax.sharding import PartitionSpec as P

HAD = 128
LANES = 128
ROWS = 16
ROUTED_SCALE = 2.5
UNIT = 1.0 / math.sqrt(HAD)
f32, bf16, i16, i32 = jnp.float32, jnp.bfloat16, jnp.int16, jnp.int32


def hadamard_table(length):
    sylvester = np.ones((1, 1), np.float32)
    while sylvester.shape[0] < length:
        sylvester = np.concatenate(
            [np.concatenate([sylvester, sylvester], 1), np.concatenate([sylvester, -sylvester], 1)],
            0,
        )
    return sylvester


def coded_order(group):
    return np.arange(HAD).reshape(HAD // group, group).T.reshape(-1)


def dot(left, right):
    return jnp.dot(left, right, preferred_element_type=f32)


def lookup(table, index):
    dims = lax.GatherDimensionNumbers(
        offset_dims=(),
        collapsed_slice_dims=(1,),
        start_index_map=(1,),
        operand_batching_dims=(0,),
        start_indices_batching_dims=(0,),
    )
    return lax.gather(
        table, index[..., None], dims, (1, 1), mode=lax.GatherScatterMode.PROMISE_IN_BOUNDS
    )


def book_tables(books):
    lead = books.shape[:-2]
    entries, group = books.shape[-2:]
    halves = entries // LANES
    turned = jnp.swapaxes(books, -1, -2).reshape(lead + (group, halves, 1, LANES))
    return jnp.broadcast_to(turned, lead + (group, halves, ROWS, LANES))


def decode_tile(code_words, table, group):
    sums = [None] * group
    for book in range(2):
        words = code_words(book).astype(i16)
        low = words & (LANES - 1)
        upper = words > LANES - 1
        found = [
            (lookup(table(book, i, 0), low), lookup(table(book, i, 1), low)) for i in range(group)
        ]
        for i in range(group):
            value = jnp.where(upper, found[i][1], found[i][0])
            sums[i] = value if book == 0 else sums[i] + value
    return sums


def decode_in(section, codes, tables, weights, order, place):
    _, mats, books, groups, hidden = codes.shape
    sections = 4
    group = tables.shape[2]
    share = groups // sections
    cols = 512

    def body(section_ref, codes_ref, tables_ref, *rest):
        out = rest[-1]
        for h in range(cols // LANES):
            lanes = slice(h * LANES, (h + 1) * LANES)
            for g in range(share // ROWS):
                tiles = decode_tile(
                    lambda c: codes_ref[0, 0, c, g * ROWS : (g + 1) * ROWS, lanes],
                    lambda c, i, half: tables_ref[0, c, i, half],
                    group,
                )
                for i in range(group):
                    at = (g * group + i) * ROWS
                    out[0, at : at + ROWS, lanes] = tiles[i]

    in_specs = [
        pl.BlockSpec(
            (1, 1, books, share, cols), lambda m, h, s: (0, m, 0, jnp.bitwise_xor(s[0], order), h)
        ),
        pl.BlockSpec((1,) + tables.shape[1:], lambda m, h, s: (m, 0, 0, 0, 0, 0)),
    ]
    operands = [section, codes, tables]
    aliases = {}
    if weights is not None:
        in_specs.append(pl.BlockSpec(memory_space=pl.ANY))
        operands.append(weights)
        aliases = {3: 0}
    return pl.pallas_call(
        body,
        grid_spec=pltpu.PrefetchScalarGridSpec(
            num_scalar_prefetch=1,
            grid=(mats, hidden // cols),
            in_specs=in_specs,
            out_specs=pl.BlockSpec((1, share * group, cols), lambda m, h, s: (m, place, h)),
        ),
        out_shape=jax.ShapeDtypeStruct((mats, groups * group, hidden), bf16),
        input_output_aliases=aliases,
        compiler_params=pltpu.CompilerParams(vmem_limit_bytes=56 << 20),
        name="decode_in",
    )(*operands)


def rotate(values, table):
    parts = []
    for b in range(values.shape[1] // HAD):
        parts.append((dot(values[:, b * HAD : (b + 1) * HAD], table) * UNIT).astype(bf16))
    return jnp.concatenate(parts, 1)


def project(pick, pieces, weights, front, middle, had):
    slots, token_total = pick.shape
    steps = len(pieces)
    width = pieces[0].shape[1]
    hidden = weights.shape[2]

    def body(*refs):
        pick_ref, *piece_refs = refs[: 1 + steps]
        weights_ref, front_ref, middle_ref, had_ref, out, total, picked = refs[1 + steps :]
        step = pl.program_id(0)
        for at in range(steps):

            @pl.when(step == at)
            def _():
                picked[...] = piece_refs[at][...]

        rows = dot(pick_ref[...], picked[...]).astype(bf16) * front_ref[0]
        turned = rotate(rows, had_ref[...])
        for m in range(2):
            part = dot(turned, weights_ref[m])
            total[m] = jnp.where(step == 0, part, total[m] + part)

        @pl.when(step == steps - 1)
        def _():
            acted = (jax.nn.silu(total[0]) * total[1]).astype(bf16)
            out[...] = rotate(acted * middle_ref[...], had_ref[...])

    whole = lambda shape: pl.BlockSpec(shape, lambda s: (0,) * len(shape))
    return pl.pallas_call(
        body,
        grid=(steps,),
        in_specs=[whole(pick.shape)]
        + [whole(p.shape) for p in pieces]
        + [
            pl.BlockSpec((2, width, hidden), lambda s: (0, s, 0)),
            pl.BlockSpec((1, 1, width), lambda s: (s, 0, 0)),
            whole(middle.shape),
            whole(had.shape),
        ],
        out_specs=whole((slots, hidden)),
        out_shape=jax.ShapeDtypeStruct((slots, hidden), bf16),
        scratch_shapes=[
            pltpu.VMEM((2, slots, hidden), f32),
            pltpu.VMEM((token_total, width), bf16),
        ],
        compiler_params=pltpu.CompilerParams(vmem_limit_bytes=32 << 20),
        name="project",
    )(pick, *pieces, weights, front, middle, had)


def produce(section, codes, tables, folded, back, had, spread, order):
    _, books, groups, width = codes.shape
    sections = 4
    group = tables.shape[1]
    slots, hidden = folded.shape
    token_total = spread.shape[0]
    cols = width // sections
    tile = 2 * LANES
    pair = 2

    def body(section_ref, codes_ref, tables_ref, folded_ref, back_ref, had_ref, spread_ref, out):
        def outcome_of(at, size):
            outcome = None
            for p in range(groups // ROWS // pair):
                strips = []
                for lane in range(at, at + size, LANES):
                    tiles = []
                    for g in range(p * pair, (p + 1) * pair):
                        tiles += decode_tile(
                            lambda c: codes_ref[0, c, g * ROWS : (g + 1) * ROWS, lane : lane + LANES],
                            lambda c, i, half: tables_ref[c, i, half],
                            group,
                        )
                    strips.append(jnp.concatenate(tiles, 0))
                depth = pair * group * ROWS
                part = dot(folded_ref[:, p * depth : (p + 1) * depth], jnp.concatenate(strips, 1))
                outcome = part if outcome is None else outcome + part
            return outcome

        def finish(outcome, at, size):
            high = outcome.astype(bf16)
            left = outcome - high.astype(f32)
            mid = left.astype(bf16)
            low = (left - mid.astype(f32)).astype(bf16)
            table = had_ref[...]
            turned = []
            for b in range(0, size, HAD):
                s = slice(b, b + HAD)
                turned.append(dot(high[:, s], table) + (dot(mid[:, s], table) + dot(low[:, s], table)))
            turned = jnp.concatenate(turned, 1) * UNIT
            result = (back_ref[:, at : at + size] * turned).astype(bf16)
            out[:, at : at + size] = dot(spread_ref[...], result).astype(bf16)

        pending = None
        at = 0
        while at < cols:
            size = min(tile, cols - at)
            outcome = outcome_of(at, size)
            if pending is not None:
                finish(*pending)
            pending = (outcome, at, size)
            at += size
        finish(*pending)

    def column(s):
        return jnp.bitwise_xor(s[0], order)

    whole = lambda shape: pl.BlockSpec(shape, lambda j, s: (0,) * len(shape))
    return pl.pallas_call(
        body,
        grid_spec=pltpu.PrefetchScalarGridSpec(
            num_scalar_prefetch=1,
            grid=(1,),
            in_specs=[
                pl.BlockSpec((1, books, groups, cols), lambda j, s: (0, 0, 0, column(s))),
                whole(tables.shape),
                whole(folded.shape),
                pl.BlockSpec((1, cols), lambda j, s: (0, column(s))),
                whole(had.shape),
                whole(spread.shape),
            ],
            out_specs=pl.BlockSpec((token_total, cols), lambda j, s: (0, j)),
        ),
        out_shape=jax.ShapeDtypeStruct((token_total, cols), bf16),
        compiler_params=pltpu.CompilerParams(vmem_limit_bytes=20 << 20),
        name="produce",
    )(section, codes, tables, folded, back, had, spread)


def swap(values, axis, stride):
    size = lax.axis_size(axis)
    return lax.ppermute(values, axis, [(i, i ^ stride) for i in range(size)])


def per_device(
    tokens,
    routes,
    scores,
    gate_up_codes,
    down_codes,
    model_signs,
    hidden_signs,
    gate_up_books,
    down_books,
):
    sections = lax.axis_size("sec")
    devices = lax.axis_size("dev")
    section = lax.axis_index("sec")
    device = lax.axis_index("dev")
    token_count, quarter = tokens.shape
    width = quarter * sections
    token_total = token_count * devices
    slots = 4 * token_count
    group = gate_up_books.shape[-1]
    chunks = 2
    half = quarter // chunks
    strides = [1 << b for b in range(devices.bit_length() - 1)]
    section_word = section.astype(i32).reshape(1)

    relative = [0]
    for stride in reversed(strides):
        relative = relative + [b ^ stride for b in relative]
    places = [0, 2, 1, 3]

    gates = (ROUTED_SCALE * scores / jnp.sum(scores, axis=1, keepdims=True)).astype(bf16)
    top = routes.shape[1]
    tables_in = book_tables(gate_up_books)
    tables_down = book_tables(down_books)
    sylvester = hadamard_table(HAD)
    had_coded = jnp.asarray(sylvester[:, coded_order(group)], bf16)
    had = jnp.asarray(sylvester, bf16)
    front = (2 * model_signs[0, 0] - 1).astype(bf16).reshape(sections, chunks, 1, half)
    front = jnp.take(front, jnp.bitwise_xor(jnp.asarray(places, i32), section.astype(i32)), axis=0)
    front = front.reshape(sections * chunks, 1, half)
    back = (2 * model_signs[0, 1] - 1).astype(f32).reshape(1, width)
    middle = (2 * hidden_signs - 1).astype(bf16)

    def fence(*values):
        return lax.optimization_barrier(values)

    facts = jnp.concatenate([routes.astype(bf16), gates], 1)
    facts = jnp.pad(facts, ((0, 0), (0, LANES - 2 * top)))
    row = jnp.concatenate([tokens, facts], 1)
    gathered = [row] + [swap(row, "dev", b) for b in relative[1 : devices // 2]]
    weights = decode_in(section_word, gate_up_codes, tables_in, None, places[0], 0)
    weights, gathered = fence(weights, gathered)
    gathered = jnp.concatenate(gathered, 0)
    first = jnp.concatenate([gathered[:, :half], gathered[:, quarter:]], 1)
    second = gathered[:, half:quarter]
    first_near = swap(first, "dev", 1)
    second_cross = swap(second, "sec", 2)
    weights, first, second = fence(weights, first, second)
    weights = decode_in(section_word, gate_up_codes, tables_in, weights, places[1], 1)
    weights, first_near, second_cross = fence(weights, first_near, second_cross)
    first = jnp.concatenate([first, first_near], 0)
    first, facts = first[:, :half], first[:, half:].astype(f32)
    first_cross = swap(first, "sec", 2)
    second_near = swap(second, "dev", 1)
    second_both = swap(second_cross, "dev", 1)
    weights = decode_in(section_word, gate_up_codes, tables_in, weights, places[2], 2)
    weights, first_cross, second_near, second_both = fence(
        weights, first_cross, second_near, second_both
    )
    second = jnp.concatenate([second, second_near], 0)
    second_cross = jnp.concatenate([second_cross, second_both], 0)
    pieces = [first, second, first_cross, second_cross]
    pieces = pieces + [swap(p, "sec", 1) for p in pieces]
    weights = decode_in(section_word, gate_up_codes, tables_in, weights, places[3], 3)

    expert = ((section - 1) * devices + device).astype(f32)
    named = facts[:, :top] == expert
    hit = jnp.any(named, axis=1)
    gate = jnp.sum(jnp.where(named, facts[:, top : 2 * top], 0.0), axis=1)
    earlier = (jnp.arange(token_total)[:, None] < jnp.arange(token_total)[None, :]).astype(f32)
    slot = jnp.sum(jnp.where(hit[:, None], earlier, 0.0), axis=0)
    slot = jnp.where(hit, slot, -1.0)
    shared = section == 0
    token_id = jnp.arange(token_total)
    own = token_id < token_count
    slot = jnp.where(shared, jnp.where(own, token_id.astype(f32), -1.0), slot)
    gate = jnp.where(shared, 1.0, gate)
    slot_id = jnp.arange(slots).astype(f32)
    pick = (slot_id[:, None] == slot[None, :]).astype(bf16)
    spread = jnp.where(slot[:, None] == slot_id[None, :], gate[:, None], 0.0).astype(bf16)


    folded = project(pick, pieces, weights, front, middle, had_coded)

    def make(order):
        return produce(section_word, down_codes, tables_down, folded, back, had, spread, order)

    def cut(values):
        return [values[:, c * half : (c + 1) * half] for c in range(chunks)]

    given = make(3)
    folded, given = fence(folded, given)
    near = swap(given, "sec", 1)
    kept = make(2)
    folded, kept, near = fence(folded, kept, near)
    crossing = cut((kept.astype(f32) + near.astype(f32)).astype(bf16))
    folded, *crossing = fence(folded, *crossing)
    crossed = [swap(c, "sec", 2) for c in crossing]
    given = make(1)
    folded, given, crossed[0] = fence(folded, given, crossed[0])
    near = swap(given, "sec", 1)
    kept = make(0)
    kept, near = fence(kept, near)
    outs = []
    for own, beside, across in zip(cut(kept), cut(near), crossed):
        total = own.astype(f32) + beside.astype(f32) + across.astype(f32)
        for stride in strides:
            rows = total.shape[0] // 2
            sent = swap(total[rows:].astype(bf16), "dev", stride)
            total = total[:rows] + sent.astype(f32)
        outs.append(total.astype(bf16))
    return jnp.concatenate(outs, 1)


def solution(mesh):
    in_specs = (
        P("dev", "sec"),
        P("dev", None),
        P("dev", None),
        P(("sec", "dev"), None, None, None, None),
        P(("sec", "dev"), None, None, None),
        P(("sec", "dev"), None, None),
        P(("sec", "dev"), None),
        P(),
        P(),
    )
    out_specs = P("dev", "sec")
    return jax.shard_map(
        per_device, mesh=mesh, in_specs=in_specs, out_specs=out_specs, check_vma=False
    )
```

```python
import math

import jax
import jax.numpy as jnp
import numpy as np
from jax import lax
from jax.experimental import pallas as pl
from jax.experimental.pallas import tpu as pltpu
from jax.sharding import PartitionSpec as P

HAD = 128
LANES = 128
ROWS = 16
ROUTED_SCALE = 2.5
UNIT = 1.0 / math.sqrt(HAD)
f32, bf16, i16, i32 = jnp.float32, jnp.bfloat16, jnp.int16, jnp.int32


def hadamard_table(length):
    sylvester = np.ones((1, 1), np.float32)
    while sylvester.shape[0] < length:
        sylvester = np.concatenate(
            [np.concatenate([sylvester, sylvester], 1), np.concatenate([sylvester, -sylvester], 1)],
            0,
        )
    return sylvester


def coded_order(group):
    return np.arange(HAD).reshape(HAD // group, group).T.reshape(-1)


def dot(left, right):
    return jnp.dot(left, right, preferred_element_type=f32)


def lookup(table, index):
    dims = lax.GatherDimensionNumbers(
        offset_dims=(),
        collapsed_slice_dims=(1,),
        start_index_map=(1,),
        operand_batching_dims=(0,),
        start_indices_batching_dims=(0,),
    )
    return lax.gather(
        table, index[..., None], dims, (1, 1), mode=lax.GatherScatterMode.PROMISE_IN_BOUNDS
    )


def book_tables(books):
    lead = books.shape[:-2]
    entries, group = books.shape[-2:]
    halves = entries // LANES
    turned = jnp.swapaxes(books, -1, -2).reshape(lead + (group, halves, 1, LANES))
    return jnp.broadcast_to(turned, lead + (group, halves, ROWS, LANES))


def decode_tile(code_words, table, group):
    sums = [None] * group
    for book in range(2):
        words = code_words(book).astype(i16)
        low = words & (LANES - 1)
        upper = words > LANES - 1
        found = [
            (lookup(table(book, i, 0), low), lookup(table(book, i, 1), low)) for i in range(group)
        ]
        for i in range(group):
            value = jnp.where(upper, found[i][1], found[i][0])
            sums[i] = value if book == 0 else sums[i] + value
    return sums


def decode_in(section, codes, tables, weights, order, place):
    _, mats, books, groups, hidden = codes.shape
    sections = 4
    group = tables.shape[2]
    share = groups // sections
    cols = 512

    def body(section_ref, codes_ref, tables_ref, *rest):
        out = rest[-1]
        for h in range(cols // LANES):
            lanes = slice(h * LANES, (h + 1) * LANES)
            for g in range(share // ROWS):
                tiles = decode_tile(
                    lambda c: codes_ref[0, 0, c, g * ROWS : (g + 1) * ROWS, lanes],
                    lambda c, i, half: tables_ref[0, c, i, half],
                    group,
                )
                for i in range(group):
                    at = (g * group + i) * ROWS
                    out[0, at : at + ROWS, lanes] = tiles[i]

    in_specs = [
        pl.BlockSpec(
            (1, 1, books, share, cols), lambda m, h, s: (0, m, 0, jnp.bitwise_xor(s[0], order), h)
        ),
        pl.BlockSpec((1,) + tables.shape[1:], lambda m, h, s: (m, 0, 0, 0, 0, 0)),
    ]
    operands = [section, codes, tables]
    aliases = {}
    if weights is not None:
        in_specs.append(pl.BlockSpec(memory_space=pl.ANY))
        operands.append(weights)
        aliases = {3: 0}
    return pl.pallas_call(
        body,
        grid_spec=pltpu.PrefetchScalarGridSpec(
            num_scalar_prefetch=1,
            grid=(mats, hidden // cols),
            in_specs=in_specs,
            out_specs=pl.BlockSpec((1, share * group, cols), lambda m, h, s: (m, place, h)),
        ),
        out_shape=jax.ShapeDtypeStruct((mats, (sections - 1) * share * group, hidden), bf16),
        input_output_aliases=aliases,
        compiler_params=pltpu.CompilerParams(vmem_limit_bytes=50 << 20),
        name="decode_in",
    )(*operands)


def rotate(values, table):
    parts = []
    for b in range(values.shape[1] // HAD):
        parts.append((dot(values[:, b * HAD : (b + 1) * HAD], table) * UNIT).astype(bf16))
    return jnp.concatenate(parts, 1)


def project(section, codes, tables, weights, pick, pieces, signs, middle, had, order, places):
    _, mats, books, groups, hidden = codes.shape
    sections = len(places)
    group = tables.shape[2]
    share = groups // sections
    slots, token_total = pick.shape
    width = pieces[0].shape[1]
    chunks = len(pieces) // sections
    stored = weights.shape[1]
    cols = 512
    per_mat = hidden // cols
    pair = 2

    def body(*refs):
        section_ref, codes_ref, tables_ref, weights_ref, pick_ref = refs[:5]
        piece_refs = refs[5 : 5 + len(pieces)]
        signs_ref, middle_ref, had_ref, out, turned, total = refs[5 + len(pieces) :]
        step = pl.program_id(0) * per_mat + pl.program_id(1)

        @pl.when(step == 0)
        def _():
            for at, piece in enumerate(piece_refs):
                quarter = jnp.bitwise_xor(section_ref[0], places[at // chunks])
                start = pl.multiple_of((quarter * chunks + at % chunks) * width, LANES)
                front = (2 * signs_ref[0, 0:1, pl.ds(start, width)] - 1).astype(bf16)
                rows = dot(pick_ref[...], piece[...]).astype(bf16) * front
                turned[:, at * width : (at + 1) * width] = rotate(rows, had_ref[...])

        part = dot(turned[:, :stored], weights_ref[0])
        depth = pair * group * ROWS
        for p in range(share // ROWS // pair):
            strips = []
            for lane in range(0, cols, LANES):
                tiles = []
                for g in range(p * pair, (p + 1) * pair):
                    tiles += decode_tile(
                        lambda c: codes_ref[
                            0, 0, c, g * ROWS : (g + 1) * ROWS, lane : lane + LANES
                        ],
                        lambda c, i, half: tables_ref[0, c, i, half],
                        group,
                    )
                strips.append(jnp.concatenate(tiles, 0))
            at = stored + p * depth
            part = part + dot(turned[:, at : at + depth], jnp.concatenate(strips, 1))
        total[step] = part

        @pl.when(step == mats * per_mat - 1)
        def _():
            for h in range(per_mat):
                lanes = slice(h * cols, (h + 1) * cols)
                acted = (jax.nn.silu(total[h]) * total[per_mat + h]).astype(bf16)
                flips = (2 * middle_ref[:, lanes] - 1).astype(bf16)
                out[:, lanes] = rotate(acted * flips, had_ref[...])

    whole = lambda shape: pl.BlockSpec(shape, lambda m, h, s: (0,) * len(shape))
    return pl.pallas_call(
        body,
        grid_spec=pltpu.PrefetchScalarGridSpec(
            num_scalar_prefetch=1,
            grid=(mats, per_mat),
            in_specs=[
                pl.BlockSpec(
                    (1, 1, books, share, cols),
                    lambda m, h, s: (0, m, 0, jnp.bitwise_xor(s[0], order), h),
                ),
                pl.BlockSpec((1,) + tables.shape[1:], lambda m, h, s: (m, 0, 0, 0, 0, 0)),
                pl.BlockSpec((1, stored, cols), lambda m, h, s: (m, 0, h)),
                whole(pick.shape),
            ]
            + [whole(p.shape) for p in pieces]
            + [whole(signs.shape), whole(middle.shape), whole(had.shape)],
            out_specs=whole((slots, hidden)),
            scratch_shapes=[
                pltpu.VMEM((slots, groups * group), bf16),
                pltpu.VMEM((mats * per_mat, slots, cols), f32),
            ],
        ),
        out_shape=jax.ShapeDtypeStruct((slots, hidden), bf16),
        compiler_params=pltpu.CompilerParams(vmem_limit_bytes=50 << 20),
        name="project",
    )(section, codes, tables, weights, pick, *pieces, signs, middle, had)


def produce(section, codes, tables, folded, signs, had, spread, order, added, dtype):
    _, books, groups, width = codes.shape
    sections = 4
    group = tables.shape[1]
    slots, hidden = folded.shape
    token_total = spread.shape[0]
    cols = width // sections
    tile = 2 * LANES
    pair = 2

    extra = [] if added is None else [added]

    def body(section_ref, codes_ref, tables_ref, folded_ref, signs_ref, had_ref, spread_ref, *rest):
        outs = rest[-2:]
        back = (2 * signs_ref[0, 1:2, :] - 1).astype(f32)

        def outcome_of(at, size):
            outcome = None
            for p in range(groups // ROWS // pair):
                strips = []
                for lane in range(at, at + size, LANES):
                    tiles = []
                    for g in range(p * pair, (p + 1) * pair):
                        tiles += decode_tile(
                            lambda c: codes_ref[0, c, g * ROWS : (g + 1) * ROWS, lane : lane + LANES],
                            lambda c, i, half: tables_ref[c, i, half],
                            group,
                        )
                    strips.append(jnp.concatenate(tiles, 0))
                depth = pair * group * ROWS
                part = dot(folded_ref[:, p * depth : (p + 1) * depth], jnp.concatenate(strips, 1))
                outcome = part if outcome is None else outcome + part
            return outcome

        def finish(outcome, at, size):
            high = outcome.astype(bf16)
            left = outcome - high.astype(f32)
            mid = left.astype(bf16)
            low = (left - mid.astype(f32)).astype(bf16)
            table = had_ref[...]
            turned = []
            for b in range(0, size, HAD):
                s = slice(b, b + HAD)
                turned.append(dot(high[:, s], table) + (dot(mid[:, s], table) + dot(low[:, s], table)))
            turned = jnp.concatenate(turned, 1) * UNIT
            result = (back[:, at : at + size] * turned).astype(bf16)
            weighted = dot(spread_ref[...], result)
            if extra:
                weighted = weighted + rest[0][:, at : at + size].astype(f32)
            for side in range(2):
                low, high = max(at, side * cols // 2), min(at + size, (side + 1) * cols // 2)
                if low < high:
                    shift = side * cols // 2
                    outs[side][:, low - shift : high - shift] = weighted[
                        :, low - at : high - at
                    ].astype(dtype)

        pending = None
        at = 0
        while at < cols:
            size = min(tile, cols - at)
            outcome = outcome_of(at, size)
            if pending is not None:
                finish(*pending)
            pending = (outcome, at, size)
            at += size
        finish(*pending)

    def column(s):
        return jnp.bitwise_xor(s[0], order)

    whole = lambda shape: pl.BlockSpec(shape, lambda j, s: (0,) * len(shape))
    return pl.pallas_call(
        body,
        grid_spec=pltpu.PrefetchScalarGridSpec(
            num_scalar_prefetch=1,
            grid=(1,),
            in_specs=[
                pl.BlockSpec((1, books, groups, cols), lambda j, s: (0, 0, 0, column(s))),
                whole(tables.shape),
                whole(folded.shape),
                pl.BlockSpec((1, 2, cols), lambda j, s: (0, 0, column(s))),
                whole(had.shape),
                whole(spread.shape),
            ]
            + [whole(e.shape) for e in extra],
            out_specs=[whole((token_total, cols // 2))] * 2,
        ),
        out_shape=[jax.ShapeDtypeStruct((token_total, cols // 2), dtype)] * 2,
        compiler_params=pltpu.CompilerParams(vmem_limit_bytes=20 << 20),
        name="produce",
    )(section, codes, tables, folded, signs, had, spread, *extra)


def swap(values, axis, stride):
    size = lax.axis_size(axis)
    return lax.ppermute(values, axis, [(i, i ^ stride) for i in range(size)])


def per_device(
    tokens,
    routes,
    scores,
    gate_up_codes,
    down_codes,
    model_signs,
    hidden_signs,
    gate_up_books,
    down_books,
):
    sections = lax.axis_size("sec")
    devices = lax.axis_size("dev")
    section = lax.axis_index("sec")
    device = lax.axis_index("dev")
    token_count, quarter = tokens.shape
    width = quarter * sections
    token_total = token_count * devices
    slots = 4 * token_count
    group = gate_up_books.shape[-1]
    chunks = 2
    half = quarter // chunks
    strides = [1 << b for b in range(devices.bit_length() - 1)]
    section_word = section.astype(i32).reshape(1)

    relative = [0]
    for stride in reversed(strides):
        relative = relative + [b ^ stride for b in relative]
    places = [0, 2, 1, 3]

    gates = (ROUTED_SCALE * scores / jnp.sum(scores, axis=1, keepdims=True)).astype(bf16)
    top = routes.shape[1]
    tables_in = book_tables(gate_up_books)
    tables_down = book_tables(down_books)
    sylvester = hadamard_table(HAD)
    had_coded = jnp.asarray(sylvester[:, coded_order(group)], bf16)
    had = jnp.asarray(sylvester, bf16)

    def fence(*values):
        return lax.optimization_barrier(values)

    facts = jnp.concatenate([routes.astype(bf16), gates], 1)
    facts = jnp.pad(facts, ((0, 0), (0, LANES - 2 * top)))
    row = jnp.concatenate([tokens, facts], 1)
    gathered = [row] + [swap(row, "dev", b) for b in relative[1 : devices // 2]]
    gathered = jnp.concatenate(gathered, 0)
    first = jnp.concatenate([gathered[:, :half], gathered[:, quarter:]], 1)
    second = gathered[:, half:quarter]
    section_word, first, second = fence(section_word, first, second)
    first_near = swap(first, "dev", 1)
    second_cross = swap(second, "sec", 2)
    weights = decode_in(section_word, gate_up_codes, tables_in, None, places[0], 0)
    weights, first_near, second_cross = fence(weights, first_near, second_cross)
    first = jnp.concatenate([first, first_near], 0)
    first, facts = first[:, :half], first[:, half:].astype(f32)
    first_cross = swap(first, "sec", 2)
    second_near = swap(second, "dev", 1)
    second_both = swap(second_cross, "dev", 1)
    weights = decode_in(section_word, gate_up_codes, tables_in, weights, places[1], 1)
    weights, first_cross, second_near, second_both = fence(
        weights, first_cross, second_near, second_both
    )
    second = jnp.concatenate([second, second_near], 0)
    second_cross = jnp.concatenate([second_cross, second_both], 0)
    pieces = [first, second, first_cross, second_cross]
    pieces = pieces + [swap(p, "sec", 1) for p in pieces]
    weights = decode_in(section_word, gate_up_codes, tables_in, weights, places[2], 2)

    expert = ((section - 1) * devices + device).astype(f32)
    named = facts[:, :top] == expert
    hit = jnp.any(named, axis=1)
    gate = jnp.sum(jnp.where(named, facts[:, top : 2 * top], 0.0), axis=1)
    earlier = (jnp.arange(token_total)[:, None] < jnp.arange(token_total)[None, :]).astype(f32)
    slot = jnp.sum(jnp.where(hit[:, None], earlier, 0.0), axis=0)
    slot = jnp.where(hit, slot, -1.0)
    shared = section == 0
    token_id = jnp.arange(token_total)
    own = token_id < token_count
    slot = jnp.where(shared, jnp.where(own, token_id.astype(f32), -1.0), slot)
    gate = jnp.where(shared, 1.0, gate)
    slot_id = jnp.arange(slots).astype(f32)
    pick = (slot_id[:, None] == slot[None, :]).astype(bf16)
    spread = jnp.where(slot[:, None] == slot_id[None, :], gate[:, None], 0.0).astype(bf16)


    folded = project(
        section_word,
        gate_up_codes,
        tables_in,
        weights,
        pick,
        pieces,
        model_signs,
        hidden_signs,
        had_coded,
        places[3],
        places,
    )

    def make(order, added=None, dtype=bf16):
        return produce(
            section_word,
            down_codes,
            tables_down,
            folded,
            model_signs,
            had,
            spread,
            order,
            added,
            dtype,
        )

    rows = token_total // 2
    far_made = jnp.concatenate(make(3), 1)
    folded, far_made = fence(folded, far_made)
    far_near = swap(far_made, "sec", 1)
    beside = jnp.concatenate(make(1), 1)
    folded, beside, far_near = fence(folded, beside, far_near)
    beside = swap(beside, "sec", 1)
    across = make(2, far_near)
    folded, beside, *across = fence(folded, beside, *across)
    first_across = swap(across[0], "sec", 2)
    second_met = swap(across[1][rows:], "dev", 1)
    first, second = make(0, beside, f32)
    first, second, second_met = fence(first, second, second_met)
    second_across = (across[1][:rows].astype(f32) + second_met.astype(f32)).astype(bf16)
    second_across = swap(second_across, "sec", 2)
    second_near = swap(second[rows:].astype(bf16), "dev", 1)
    first = first + first_across.astype(f32)
    first_near = swap(first[rows:].astype(bf16), "dev", 1)
    first = first[:rows] + first_near.astype(f32)
    second = second[:rows] + second_near.astype(f32) + second_across.astype(f32)
    outs = []
    for total in (first, second):
        for stride in strides[1:]:
            rows = total.shape[0] // 2
            sent = swap(total[rows:].astype(bf16), "dev", stride)
            total = total[:rows] + sent.astype(f32)
        outs.append(total.astype(bf16))
    return jnp.concatenate(outs, 1)


def solution(mesh):
    in_specs = (
        P("dev", "sec"),
        P("dev", None),
        P("dev", None),
        P(("sec", "dev"), None, None, None, None),
        P(("sec", "dev"), None, None, None),
        P(("sec", "dev"), None, None),
        P(("sec", "dev"), None),
        P(),
        P(),
    )
    out_specs = P("dev", "sec")
    return jax.shard_map(
        per_device, mesh=mesh, in_specs=in_specs, out_specs=out_specs, check_vma=False
    )
```

```python
import math

import jax
import jax.numpy as jnp
import numpy as np
from jax import lax
from jax.experimental import pallas as pl
from jax.experimental.pallas import tpu as pltpu
from jax.sharding import PartitionSpec as P

HAD = 128
LANES = 128
ROWS = 16
ROUTED_SCALE = 2.5
UNIT = 1.0 / math.sqrt(HAD)
f32, bf16, i16, i32 = jnp.float32, jnp.bfloat16, jnp.int16, jnp.int32


def hadamard_table(length):
    sylvester = np.ones((1, 1), np.float32)
    while sylvester.shape[0] < length:
        sylvester = np.concatenate(
            [np.concatenate([sylvester, sylvester], 1), np.concatenate([sylvester, -sylvester], 1)],
            0,
        )
    return sylvester


def coded_order(group):
    return np.arange(HAD).reshape(HAD // group, group).T.reshape(-1)


def dot(left, right):
    return jnp.dot(left, right, preferred_element_type=f32)


def lookup(table, index):
    dims = lax.GatherDimensionNumbers(
        offset_dims=(),
        collapsed_slice_dims=(1,),
        start_index_map=(1,),
        operand_batching_dims=(0,),
        start_indices_batching_dims=(0,),
    )
    return lax.gather(
        table, index[..., None], dims, (1, 1), mode=lax.GatherScatterMode.PROMISE_IN_BOUNDS
    )


def book_tables(books):
    lead = books.shape[:-2]
    entries, group = books.shape[-2:]
    halves = entries // LANES
    turned = jnp.swapaxes(books, -1, -2).reshape(lead + (group, halves, 1, LANES))
    return jnp.broadcast_to(turned, lead + (group, halves, ROWS, LANES))


def decode_tile(code_words, table, group):
    sums = [None] * group
    for book in range(2):
        words = code_words(book).astype(i16)
        low = words & (LANES - 1)
        upper = words > LANES - 1
        found = [
            (lookup(table(book, i, 0), low), lookup(table(book, i, 1), low)) for i in range(group)
        ]
        for i in range(group):
            value = jnp.where(upper, found[i][1], found[i][0])
            sums[i] = value if book == 0 else sums[i] + value
    return sums


def decode_in(section, codes, tables, weights, piece, cols, stored):
    _, mats, books, groups, hidden = codes.shape
    sections = stored + 1
    group = tables.shape[2]
    share = groups // sections
    per_mat = hidden // cols
    mat, block = piece // per_mat, piece % per_mat

    def body(section_ref, codes_ref, tables_ref, *rest):
        out = rest[-1]
        for h in range(cols // LANES):
            lanes = slice(h * LANES, (h + 1) * LANES)
            for g in range(share // ROWS):
                tiles = decode_tile(
                    lambda c: codes_ref[0, 0, c, g * ROWS : (g + 1) * ROWS, lanes],
                    lambda c, i, half: tables_ref[0, c, i, half],
                    group,
                )
                for i in range(group):
                    at = (g * group + i) * ROWS
                    out[0, at : at + ROWS, lanes] = tiles[i]

    def source(j, s):
        return (0, mat, 0, jnp.bitwise_xor(s[0], (j % 2) * 2 + j // 2), block)

    in_specs = [
        pl.BlockSpec((1, 1, books, share, cols), source),
        pl.BlockSpec((1,) + tables.shape[1:], lambda j, s: (mat, 0, 0, 0, 0, 0)),
    ]
    operands = [section, codes, tables]
    aliases = {}
    if weights is not None:
        in_specs.append(pl.BlockSpec(memory_space=pl.ANY))
        operands.append(weights)
        aliases = {3: 0}
    return pl.pallas_call(
        body,
        grid_spec=pltpu.PrefetchScalarGridSpec(
            num_scalar_prefetch=1,
            grid=(stored,),
            in_specs=in_specs,
            out_specs=pl.BlockSpec((1, share * group, cols), lambda j, s: (mat, j, block)),
        ),
        out_shape=jax.ShapeDtypeStruct((mats, stored * share * group, hidden), bf16),
        input_output_aliases=aliases,
        compiler_params=pltpu.CompilerParams(vmem_limit_bytes=50 << 20),
        name="decode_in",
    )(*operands)


def rotate(values, table):
    parts = []
    for b in range(values.shape[1] // HAD):
        parts.append((dot(values[:, b * HAD : (b + 1) * HAD], table) * UNIT).astype(bf16))
    return jnp.concatenate(parts, 1)


def project(section, codes, tables, weights, pick, pieces, signs, middle, had, order, places):
    _, mats, books, groups, hidden = codes.shape
    sections = len(places)
    group = tables.shape[2]
    share = groups // sections
    slots, token_total = pick.shape
    width = pieces[0].shape[1]
    chunks = len(pieces) // sections
    stored = weights.shape[1]
    cols = 512
    per_mat = hidden // cols
    pair = 2

    def body(*refs):
        section_ref, codes_ref, tables_ref, weights_ref, pick_ref = refs[:5]
        piece_refs = refs[5 : 5 + len(pieces)]
        signs_ref, middle_ref, had_ref, out, turned, total = refs[5 + len(pieces) :]
        step = pl.program_id(0) * per_mat + pl.program_id(1)

        @pl.when(step == 0)
        def _():
            for at, piece in enumerate(piece_refs):
                quarter = jnp.bitwise_xor(section_ref[0], places[at // chunks])
                start = pl.multiple_of((quarter * chunks + at % chunks) * width, LANES)
                front = (2 * signs_ref[0, 0:1, pl.ds(start, width)] - 1).astype(bf16)
                rows = dot(pick_ref[...], piece[...]).astype(bf16) * front
                turned[:, at * width : (at + 1) * width] = rotate(rows, had_ref[...])

        part = dot(turned[:, :stored], weights_ref[0])
        depth = pair * group * ROWS
        for p in range(share // ROWS // pair):
            strips = []
            for lane in range(0, cols, LANES):
                tiles = []
                for g in range(p * pair, (p + 1) * pair):
                    tiles += decode_tile(
                        lambda c: codes_ref[
                            0, 0, c, g * ROWS : (g + 1) * ROWS, lane : lane + LANES
                        ],
                        lambda c, i, half: tables_ref[0, c, i, half],
                        group,
                    )
                strips.append(jnp.concatenate(tiles, 0))
            at = stored + p * depth
            part = part + dot(turned[:, at : at + depth], jnp.concatenate(strips, 1))
        total[step] = part

        @pl.when(step == mats * per_mat - 1)
        def _():
            for h in range(per_mat):
                lanes = slice(h * cols, (h + 1) * cols)
                acted = (jax.nn.silu(total[h]) * total[per_mat + h]).astype(bf16)
                flips = (2 * middle_ref[:, lanes] - 1).astype(bf16)
                out[:, lanes] = rotate(acted * flips, had_ref[...])

    whole = lambda shape: pl.BlockSpec(shape, lambda m, h, s: (0,) * len(shape))
    return pl.pallas_call(
        body,
        grid_spec=pltpu.PrefetchScalarGridSpec(
            num_scalar_prefetch=1,
            grid=(mats, per_mat),
            in_specs=[
                pl.BlockSpec(
                    (1, 1, books, share, cols),
                    lambda m, h, s: (0, m, 0, jnp.bitwise_xor(s[0], order), h),
                ),
                pl.BlockSpec((1,) + tables.shape[1:], lambda m, h, s: (m, 0, 0, 0, 0, 0)),
                pl.BlockSpec((1, stored, cols), lambda m, h, s: (m, 0, h)),
                whole(pick.shape),
            ]
            + [whole(p.shape) for p in pieces]
            + [whole(signs.shape), whole(middle.shape), whole(had.shape)],
            out_specs=whole((slots, hidden)),
            scratch_shapes=[
                pltpu.VMEM((slots, groups * group), bf16),
                pltpu.VMEM((mats * per_mat, slots, cols), f32),
            ],
        ),
        out_shape=jax.ShapeDtypeStruct((slots, hidden), bf16),
        compiler_params=pltpu.CompilerParams(vmem_limit_bytes=50 << 20),
        name="project",
    )(section, codes, tables, weights, pick, *pieces, signs, middle, had)


def produce(section, codes, tables, folded, signs, had, spread, order, cols, at_col, dtype):
    _, books, groups, width = codes.shape
    sections = 4
    group = tables.shape[1]
    slots, hidden = folded.shape
    token_total = spread.shape[0]
    per_quarter = width // sections // cols
    tile = 2 * LANES
    pair = 2

    def body(section_ref, codes_ref, tables_ref, folded_ref, signs_ref, had_ref, spread_ref, out):
        back = (2 * signs_ref[0, 1:2, :] - 1).astype(f32)

        def outcome_of(at, size):
            outcome = None
            for p in range(groups // ROWS // pair):
                strips = []
                for lane in range(at, at + size, LANES):
                    tiles = []
                    for g in range(p * pair, (p + 1) * pair):
                        tiles += decode_tile(
                            lambda c: codes_ref[0, c, g * ROWS : (g + 1) * ROWS, lane : lane + LANES],
                            lambda c, i, half: tables_ref[c, i, half],
                            group,
                        )
                    strips.append(jnp.concatenate(tiles, 0))
                depth = pair * group * ROWS
                part = dot(folded_ref[:, p * depth : (p + 1) * depth], jnp.concatenate(strips, 1))
                outcome = part if outcome is None else outcome + part
            return outcome

        def finish(outcome, at, size):
            high = outcome.astype(bf16)
            left = outcome - high.astype(f32)
            mid = left.astype(bf16)
            low = (left - mid.astype(f32)).astype(bf16)
            table = had_ref[...]
            turned = []
            for b in range(0, size, HAD):
                s = slice(b, b + HAD)
                turned.append(dot(high[:, s], table) + (dot(mid[:, s], table) + dot(low[:, s], table)))
            turned = jnp.concatenate(turned, 1) * UNIT
            result = (back[:, at : at + size] * turned).astype(bf16)
            out[:, at : at + size] = dot(spread_ref[...], result).astype(dtype)

        pending = None
        at = 0
        while at < cols:
            size = min(tile, cols - at)
            outcome = outcome_of(at, size)
            if pending is not None:
                finish(*pending)
            pending = (outcome, at, size)
            at += size
        finish(*pending)

    def column(s):
        return jnp.bitwise_xor(s[0], order) * per_quarter + at_col

    whole = lambda shape: pl.BlockSpec(shape, lambda j, s: (0,) * len(shape))
    return pl.pallas_call(
        body,
        grid_spec=pltpu.PrefetchScalarGridSpec(
            num_scalar_prefetch=1,
            grid=(1,),
            in_specs=[
                pl.BlockSpec((1, books, groups, cols), lambda j, s: (0, 0, 0, column(s))),
                whole(tables.shape),
                whole(folded.shape),
                pl.BlockSpec((1, 2, cols), lambda j, s: (0, 0, column(s))),
                whole(had.shape),
                whole(spread.shape),
            ],
            out_specs=whole((token_total, cols)),
        ),
        out_shape=jax.ShapeDtypeStruct((token_total, cols), dtype),
        compiler_params=pltpu.CompilerParams(vmem_limit_bytes=20 << 20),
        name="produce",
    )(section, codes, tables, folded, signs, had, spread)


def swap(values, axis, stride):
    size = lax.axis_size(axis)
    return lax.ppermute(values, axis, [(i, i ^ stride) for i in range(size)])


def per_device(
    tokens,
    routes,
    scores,
    gate_up_codes,
    down_codes,
    model_signs,
    hidden_signs,
    gate_up_books,
    down_books,
):
    sections = lax.axis_size("sec")
    devices = lax.axis_size("dev")
    section = lax.axis_index("sec")
    device = lax.axis_index("dev")
    token_count, quarter = tokens.shape
    width = quarter * sections
    token_total = token_count * devices
    slots = 4 * token_count
    group = gate_up_books.shape[-1]
    chunks = 2
    half = quarter // chunks
    strides = [1 << b for b in range(devices.bit_length() - 1)]
    section_word = section.astype(i32).reshape(1)

    relative = [0]
    for stride in reversed(strides):
        relative = relative + [b ^ stride for b in relative]
    places = [0, 2, 1, 3]

    gates = (ROUTED_SCALE * scores / jnp.sum(scores, axis=1, keepdims=True)).astype(bf16)
    top = routes.shape[1]
    tables_in = book_tables(gate_up_books)
    tables_down = book_tables(down_books)
    sylvester = hadamard_table(HAD)
    had_coded = jnp.asarray(sylvester[:, coded_order(group)], bf16)
    had = jnp.asarray(sylvester, bf16)

    def fence(*values):
        return lax.optimization_barrier(values)

    facts = jnp.concatenate([routes.astype(bf16), gates], 1)
    facts = jnp.pad(facts, ((0, 0), (0, LANES - 2 * top)))
    row = jnp.concatenate([tokens, facts], 1)
    gathered = [row] + [swap(row, "dev", b) for b in relative[1 : devices // 2]]

    def piece_of(stack, piece):
        return decode_in(
            section_word, gate_up_codes, tables_in, stack, piece, hidden // 2, sections - 1
        )

    hidden = gate_up_codes.shape[-1]
    weights = piece_of(None, 0)
    weights, gathered = fence(weights, gathered)
    gathered = jnp.concatenate(gathered, 0)
    first = jnp.concatenate([gathered[:, :half], gathered[:, quarter:]], 1)
    second = gathered[:, half:quarter]
    weights, first, second = fence(weights, first, second)
    first_near = swap(first, "dev", 1)
    second_cross = swap(second, "sec", 2)
    weights = piece_of(weights, 1)
    weights, first_near, second_cross = fence(weights, first_near, second_cross)
    first = jnp.concatenate([first, first_near], 0)
    first, facts = first[:, :half], first[:, half:].astype(f32)
    first_cross = swap(first, "sec", 2)
    second_near = swap(second, "dev", 1)
    second_both = swap(second_cross, "dev", 1)
    weights = piece_of(weights, 2)
    weights, first_cross, second_near, second_both = fence(
        weights, first_cross, second_near, second_both
    )
    second = jnp.concatenate([second, second_near], 0)
    second_cross = jnp.concatenate([second_cross, second_both], 0)
    pieces = [first, second, first_cross, second_cross]
    pieces = pieces + [swap(p, "sec", 1) for p in pieces]
    weights = piece_of(weights, 3)

    expert = ((section - 1) * devices + device).astype(f32)
    named = facts[:, :top] == expert
    hit = jnp.any(named, axis=1)
    gate = jnp.sum(jnp.where(named, facts[:, top : 2 * top], 0.0), axis=1)
    earlier = (jnp.arange(token_total)[:, None] < jnp.arange(token_total)[None, :]).astype(f32)
    slot = jnp.sum(jnp.where(hit[:, None], earlier, 0.0), axis=0)
    slot = jnp.where(hit, slot, -1.0)
    shared = section == 0
    token_id = jnp.arange(token_total)
    own = token_id < token_count
    slot = jnp.where(shared, jnp.where(own, token_id.astype(f32), -1.0), slot)
    gate = jnp.where(shared, 1.0, gate)
    slot_id = jnp.arange(slots).astype(f32)
    pick = (slot_id[:, None] == slot[None, :]).astype(bf16)
    spread = jnp.where(slot[:, None] == slot_id[None, :], gate[:, None], 0.0).astype(bf16)


    folded = project(
        section_word,
        gate_up_codes,
        tables_in,
        weights,
        pick,
        pieces,
        model_signs,
        hidden_signs,
        had_coded,
        places[3],
        places,
    )

    def make(order, cols=quarter, at_col=0, dtype=bf16):
        return produce(
            section_word,
            down_codes,
            tables_down,
            folded,
            model_signs,
            had,
            spread,
            order,
            cols,
            at_col,
            dtype,
        )

    rows = token_total // 2
    given = make(3)
    folded, given = fence(folded, given)
    given = swap(given, "sec", 1)
    across = make(2)
    folded, across, given = fence(folded, across, given)
    across = across.astype(f32) + given.astype(f32)
    early = half // LANES // 2 * LANES
    first_across = [across[:, :early].astype(bf16), across[:, early:half].astype(bf16)]
    second_met = across[rows:, half:].astype(bf16)
    second_kept = across[:rows, half:].astype(bf16)
    folded, *first_across, second_met, second_kept = fence(
        folded, *first_across, second_met, second_kept
    )
    first_across = [swap(f, "sec", 2) for f in first_across]
    second_met = swap(second_met, "dev", 1)
    beside = make(1)
    folded, beside, second_met, first_across[0] = fence(
        folded, beside, second_met, first_across[0]
    )
    beside = swap(beside, "sec", 1)
    second_across = (second_kept.astype(f32) + second_met.astype(f32)).astype(bf16)
    second_across = swap(second_across, "sec", 2)
    second = make(0, half, 1, f32)
    folded, second, beside = fence(folded, second, beside)
    second = second + beside[:, half:].astype(f32)
    second_near = swap(second[rows:].astype(bf16), "dev", 1)
    first = make(0, half, 0, f32)
    first, second_near = fence(first, second_near)
    first_across = jnp.concatenate(first_across, 1)
    first = first + beside[:, :half].astype(f32) + first_across.astype(f32)
    first_near = swap(first[rows:].astype(bf16), "dev", 1)
    second = second[:rows] + second_near.astype(f32) + second_across.astype(f32)
    first = first[:rows] + first_near.astype(f32)
    outs = []
    for total in (first, second):
        for stride in strides[1:]:
            rows = total.shape[0] // 2
            sent = swap(total[rows:].astype(bf16), "dev", stride)
            total = total[:rows] + sent.astype(f32)
        outs.append(total.astype(bf16))
    return jnp.concatenate(outs, 1)


def solution(mesh):
    in_specs = (
        P("dev", "sec"),
        P("dev", None),
        P("dev", None),
        P(("sec", "dev"), None, None, None, None),
        P(("sec", "dev"), None, None, None),
        P(("sec", "dev"), None, None),
        P(("sec", "dev"), None),
        P(),
        P(),
    )
    out_specs = P("dev", "sec")
    return jax.shard_map(
        per_device, mesh=mesh, in_specs=in_specs, out_specs=out_specs, check_vma=False
    )
```

```python
import math

import jax
import jax.numpy as jnp
import numpy as np
from jax import lax
from jax.experimental import pallas as pl
from jax.experimental.pallas import tpu as pltpu
from jax.sharding import PartitionSpec as P

HAD = 128
LANES = 128
ROWS = 16
ROUTED_SCALE = 2.5
UNIT = 1.0 / math.sqrt(HAD)
f32, bf16, i16, i32 = jnp.float32, jnp.bfloat16, jnp.int16, jnp.int32


def hadamard_table(length):
    sylvester = np.ones((1, 1), np.float32)
    while sylvester.shape[0] < length:
        sylvester = np.concatenate(
            [np.concatenate([sylvester, sylvester], 1), np.concatenate([sylvester, -sylvester], 1)],
            0,
        )
    return sylvester


def coded_order(group):
    return np.arange(HAD).reshape(HAD // group, group).T.reshape(-1)


def dot(left, right):
    return jnp.dot(left, right, preferred_element_type=f32)


def lookup(table, index):
    dims = lax.GatherDimensionNumbers(
        offset_dims=(),
        collapsed_slice_dims=(1,),
        start_index_map=(1,),
        operand_batching_dims=(0,),
        start_indices_batching_dims=(0,),
    )
    return lax.gather(
        table, index[..., None], dims, (1, 1), mode=lax.GatherScatterMode.PROMISE_IN_BOUNDS
    )


def book_tables(books):
    lead = books.shape[:-2]
    entries, group = books.shape[-2:]
    halves = entries // LANES
    turned = jnp.swapaxes(books, -1, -2).reshape(lead + (group, halves, 1, LANES))
    return jnp.broadcast_to(turned, lead + (group, halves, ROWS, LANES))


def decode_tile(code_words, table, group):
    sums = [None] * group
    for book in range(2):
        words = code_words(book).astype(i16)
        low = words & (LANES - 1)
        upper = words > LANES - 1
        found = [
            (lookup(table(book, i, 0), low), lookup(table(book, i, 1), low)) for i in range(group)
        ]
        for i in range(group):
            value = jnp.where(upper, found[i][1], found[i][0])
            sums[i] = value if book == 0 else sums[i] + value
    return sums


def decode_in(section, codes, tables, weights, piece, cols, stored):
    _, mats, books, groups, hidden = codes.shape
    sections = stored + 1
    group = tables.shape[2]
    share = groups // sections
    per_mat = hidden // cols
    mat, block = piece // per_mat, piece % per_mat

    def body(section_ref, codes_ref, tables_ref, *rest):
        out = rest[-1]
        for h in range(cols // LANES):
            lanes = slice(h * LANES, (h + 1) * LANES)
            for g in range(share // ROWS):
                tiles = decode_tile(
                    lambda c: codes_ref[0, 0, c, g * ROWS : (g + 1) * ROWS, lanes],
                    lambda c, i, half: tables_ref[0, c, i, half],
                    group,
                )
                for i in range(group):
                    at = (g * group + i) * ROWS
                    out[0, at : at + ROWS, lanes] = tiles[i]

    def source(j, s):
        return (0, mat, 0, jnp.bitwise_xor(s[0], (j % 2) * 2 + j // 2), block)

    in_specs = [
        pl.BlockSpec((1, 1, books, share, cols), source),
        pl.BlockSpec((1,) + tables.shape[1:], lambda j, s: (mat, 0, 0, 0, 0, 0)),
    ]
    operands = [section, codes, tables]
    aliases = {}
    if weights is not None:
        in_specs.append(pl.BlockSpec(memory_space=pl.ANY))
        operands.append(weights)
        aliases = {3: 0}
    return pl.pallas_call(
        body,
        grid_spec=pltpu.PrefetchScalarGridSpec(
            num_scalar_prefetch=1,
            grid=(stored,),
            in_specs=in_specs,
            out_specs=pl.BlockSpec((1, share * group, cols), lambda j, s: (mat, j, block)),
        ),
        out_shape=jax.ShapeDtypeStruct((mats, stored * share * group, hidden), bf16),
        input_output_aliases=aliases,
        compiler_params=pltpu.CompilerParams(vmem_limit_bytes=50 << 20),
        name="decode_in",
    )(*operands)


def rotate(values, table):
    parts = []
    for b in range(values.shape[1] // HAD):
        parts.append((dot(values[:, b * HAD : (b + 1) * HAD], table) * UNIT).astype(bf16))
    return jnp.concatenate(parts, 1)


def project(section, codes, tables, weights, pick, pieces, signs, middle, had, order, places):
    _, mats, books, groups, hidden = codes.shape
    sections = len(places)
    group = tables.shape[2]
    share = groups // sections
    slots, token_total = pick.shape
    width = pieces[0].shape[1]
    chunks = len(pieces) // sections
    stored = weights.shape[1]
    cols = 512
    per_mat = hidden // cols
    pair = 2

    def body(*refs):
        section_ref, codes_ref, tables_ref, weights_ref, pick_ref = refs[:5]
        piece_refs = refs[5 : 5 + len(pieces)]
        signs_ref, middle_ref, had_ref, out, turned, total = refs[5 + len(pieces) :]
        step = pl.program_id(0) * per_mat + pl.program_id(1)

        @pl.when(step == 0)
        def _():
            for at, piece in enumerate(piece_refs):
                quarter = jnp.bitwise_xor(section_ref[0], places[at // chunks])
                start = pl.multiple_of((quarter * chunks + at % chunks) * width, LANES)
                front = (2 * signs_ref[0, 0:1, pl.ds(start, width)] - 1).astype(bf16)
                rows = dot(pick_ref[...], piece[...]).astype(bf16) * front
                turned[:, at * width : (at + 1) * width] = rotate(rows, had_ref[...])

        part = dot(turned[:, :stored], weights_ref[0])
        depth = pair * group * ROWS
        for p in range(share // ROWS // pair):
            strips = []
            for lane in range(0, cols, LANES):
                tiles = []
                for g in range(p * pair, (p + 1) * pair):
                    tiles += decode_tile(
                        lambda c: codes_ref[
                            0, 0, c, g * ROWS : (g + 1) * ROWS, lane : lane + LANES
                        ],
                        lambda c, i, half: tables_ref[0, c, i, half],
                        group,
                    )
                strips.append(jnp.concatenate(tiles, 0))
            at = stored + p * depth
            part = part + dot(turned[:, at : at + depth], jnp.concatenate(strips, 1))
        total[step] = part

        @pl.when(step == mats * per_mat - 1)
        def _():
            for h in range(per_mat):
                lanes = slice(h * cols, (h + 1) * cols)
                acted = (jax.nn.silu(total[h]) * total[per_mat + h]).astype(bf16)
                flips = (2 * middle_ref[:, lanes] - 1).astype(bf16)
                out[:, lanes] = rotate(acted * flips, had_ref[...])

    whole = lambda shape: pl.BlockSpec(shape, lambda m, h, s: (0,) * len(shape))
    return pl.pallas_call(
        body,
        grid_spec=pltpu.PrefetchScalarGridSpec(
            num_scalar_prefetch=1,
            grid=(mats, per_mat),
            in_specs=[
                pl.BlockSpec(
                    (1, 1, books, share, cols),
                    lambda m, h, s: (0, m, 0, jnp.bitwise_xor(s[0], order), h),
                ),
                pl.BlockSpec((1,) + tables.shape[1:], lambda m, h, s: (m, 0, 0, 0, 0, 0)),
                pl.BlockSpec((1, stored, cols), lambda m, h, s: (m, 0, h)),
                whole(pick.shape),
            ]
            + [whole(p.shape) for p in pieces]
            + [whole(signs.shape), whole(middle.shape), whole(had.shape)],
            out_specs=whole((slots, hidden)),
            scratch_shapes=[
                pltpu.VMEM((slots, groups * group), bf16),
                pltpu.VMEM((mats * per_mat, slots, cols), f32),
            ],
        ),
        out_shape=jax.ShapeDtypeStruct((slots, hidden), bf16),
        compiler_params=pltpu.CompilerParams(vmem_limit_bytes=50 << 20),
        name="project",
    )(section, codes, tables, weights, pick, *pieces, signs, middle, had)


def produce(section, codes, tables, folded, signs, had, spread, order, cols, at_col, dtype):
    _, books, groups, width = codes.shape
    sections = 4
    group = tables.shape[1]
    slots, hidden = folded.shape
    token_total = spread.shape[0]
    quarter = width // sections
    tile = 2 * LANES
    pair = 2

    def body(section_ref, codes_ref, tables_ref, folded_ref, signs_ref, had_ref, spread_ref, out):
        back = (2 * signs_ref[0, 1:2, :] - 1).astype(f32)

        def outcome_of(at, size):
            outcome = None
            for p in range(groups // ROWS // pair):
                strips = []
                for lane in range(at, at + size, LANES):
                    tiles = []
                    for g in range(p * pair, (p + 1) * pair):
                        tiles += decode_tile(
                            lambda c: codes_ref[0, c, g * ROWS : (g + 1) * ROWS, lane : lane + LANES],
                            lambda c, i, half: tables_ref[c, i, half],
                            group,
                        )
                    strips.append(jnp.concatenate(tiles, 0))
                depth = pair * group * ROWS
                part = dot(folded_ref[:, p * depth : (p + 1) * depth], jnp.concatenate(strips, 1))
                outcome = part if outcome is None else outcome + part
            return outcome

        def finish(outcome, at, size):
            high = outcome.astype(bf16)
            left = outcome - high.astype(f32)
            mid = left.astype(bf16)
            low = (left - mid.astype(f32)).astype(bf16)
            table = had_ref[...]
            turned = []
            for b in range(0, size, HAD):
                s = slice(b, b + HAD)
                turned.append(dot(high[:, s], table) + (dot(mid[:, s], table) + dot(low[:, s], table)))
            turned = jnp.concatenate(turned, 1) * UNIT
            result = (back[:, at : at + size] * turned).astype(bf16)
            out[:, at : at + size] = dot(spread_ref[...], result).astype(dtype)

        pending = None
        at = 0
        while at < cols:
            size = min(tile, cols - at)
            outcome = outcome_of(at, size)
            if pending is not None:
                finish(*pending)
            pending = (outcome, at, size)
            at += size
        finish(*pending)

    def column(s):
        return pl.multiple_of(jnp.bitwise_xor(s[0], order) * quarter + at_col, LANES)

    whole = lambda shape: pl.BlockSpec(shape, lambda j, s: (0,) * len(shape))
    return pl.pallas_call(
        body,
        grid_spec=pltpu.PrefetchScalarGridSpec(
            num_scalar_prefetch=1,
            grid=(1,),
            in_specs=[
                pl.BlockSpec(
                    tuple(pl.Element(n) for n in (1, books, groups, cols)),
                    lambda j, s: (0, 0, 0, column(s)),
                ),
                whole(tables.shape),
                whole(folded.shape),
                pl.BlockSpec(
                    tuple(pl.Element(n) for n in (1, 2, cols)), lambda j, s: (0, 0, column(s))
                ),
                whole(had.shape),
                whole(spread.shape),
            ],
            out_specs=whole((token_total, cols)),
        ),
        out_shape=jax.ShapeDtypeStruct((token_total, cols), dtype),
        compiler_params=pltpu.CompilerParams(vmem_limit_bytes=20 << 20),
        name="produce",
    )(section, codes, tables, folded, signs, had, spread)


def swap(values, axis, stride):
    size = lax.axis_size(axis)
    return lax.ppermute(values, axis, [(i, i ^ stride) for i in range(size)])


def per_device(
    tokens,
    routes,
    scores,
    gate_up_codes,
    down_codes,
    model_signs,
    hidden_signs,
    gate_up_books,
    down_books,
):
    sections = lax.axis_size("sec")
    devices = lax.axis_size("dev")
    section = lax.axis_index("sec")
    device = lax.axis_index("dev")
    token_count, quarter = tokens.shape
    width = quarter * sections
    token_total = token_count * devices
    slots = 4 * token_count
    group = gate_up_books.shape[-1]
    chunks = 2
    half = quarter // chunks
    strides = [1 << b for b in range(devices.bit_length() - 1)]
    section_word = section.astype(i32).reshape(1)

    relative = [0]
    for stride in reversed(strides):
        relative = relative + [b ^ stride for b in relative]
    places = [0, 2, 1, 3]

    gates = (ROUTED_SCALE * scores / jnp.sum(scores, axis=1, keepdims=True)).astype(bf16)
    top = routes.shape[1]
    tables_in = book_tables(gate_up_books)
    tables_down = book_tables(down_books)
    sylvester = hadamard_table(HAD)
    had_coded = jnp.asarray(sylvester[:, coded_order(group)], bf16)
    had = jnp.asarray(sylvester, bf16)

    def fence(*values):
        return lax.optimization_barrier(values)

    facts = jnp.concatenate([routes.astype(bf16), gates], 1)
    facts = jnp.pad(facts, ((0, 0), (0, LANES - 2 * top)))
    row = jnp.concatenate([tokens, facts], 1)
    gathered = [row] + [swap(row, "dev", b) for b in relative[1 : devices // 2]]

    def piece_of(stack, piece):
        return decode_in(
            section_word, gate_up_codes, tables_in, stack, piece, hidden // 2, sections - 1
        )

    hidden = gate_up_codes.shape[-1]
    weights = piece_of(None, 0)
    weights, gathered = fence(weights, gathered)
    gathered = jnp.concatenate(gathered, 0)
    first = jnp.concatenate([gathered[:, :half], gathered[:, quarter:]], 1)
    second = gathered[:, half:quarter]
    weights, first, second = fence(weights, first, second)
    first_near = swap(first, "dev", 1)
    second_cross = swap(second, "sec", 2)
    weights = piece_of(weights, 1)
    weights, first_near, second_cross = fence(weights, first_near, second_cross)
    first = jnp.concatenate([first, first_near], 0)
    first, facts = first[:, :half], first[:, half:].astype(f32)
    first_cross = swap(first, "sec", 2)
    second_near = swap(second, "dev", 1)
    second_both = swap(second_cross, "dev", 1)
    weights = piece_of(weights, 2)
    weights, first_cross, second_near, second_both = fence(
        weights, first_cross, second_near, second_both
    )
    second = jnp.concatenate([second, second_near], 0)
    second_cross = jnp.concatenate([second_cross, second_both], 0)
    pieces = [first, second, first_cross, second_cross]
    pieces = pieces + [swap(p, "sec", 1) for p in pieces]
    weights = piece_of(weights, 3)

    expert = ((section - 1) * devices + device).astype(f32)
    named = facts[:, :top] == expert
    hit = jnp.any(named, axis=1)
    gate = jnp.sum(jnp.where(named, facts[:, top : 2 * top], 0.0), axis=1)
    earlier = (jnp.arange(token_total)[:, None] < jnp.arange(token_total)[None, :]).astype(f32)
    slot = jnp.sum(jnp.where(hit[:, None], earlier, 0.0), axis=0)
    slot = jnp.where(hit, slot, -1.0)
    shared = section == 0
    token_id = jnp.arange(token_total)
    own = token_id < token_count
    slot = jnp.where(shared, jnp.where(own, token_id.astype(f32), -1.0), slot)
    gate = jnp.where(shared, 1.0, gate)
    slot_id = jnp.arange(slots).astype(f32)
    pick = (slot_id[:, None] == slot[None, :]).astype(bf16)
    spread = jnp.where(slot[:, None] == slot_id[None, :], gate[:, None], 0.0).astype(bf16)


    folded = project(
        section_word,
        gate_up_codes,
        tables_in,
        weights,
        pick,
        pieces,
        model_signs,
        hidden_signs,
        had_coded,
        places[3],
        places,
    )

    def make(order, cols=quarter, at_col=0, dtype=bf16):
        return produce(
            section_word,
            down_codes,
            tables_down,
            folded,
            model_signs,
            had,
            spread,
            order,
            cols,
            at_col,
            dtype,
        )

    rows = token_total // 2
    given = make(3)
    folded, given = fence(folded, given)
    given = swap(given, "sec", 1)
    across = make(2)
    folded, across, given = fence(folded, across, given)
    across = across.astype(f32) + given.astype(f32)
    lead = quarter // LANES // 3 * LANES
    first_across = across[:, :lead].astype(bf16)
    second_met = across[rows:, lead:].astype(bf16)
    second_kept = across[:rows, lead:].astype(bf16)
    folded, first_across, second_met, second_kept = fence(
        folded, first_across, second_met, second_kept
    )
    first_across = swap(first_across, "sec", 2)
    second_met = swap(second_met, "dev", 1)
    beside = make(1)
    folded, beside, second_met, first_across = fence(folded, beside, second_met, first_across)
    beside = swap(beside, "sec", 1)
    second_across = (second_kept.astype(f32) + second_met.astype(f32)).astype(bf16)
    second_across = swap(second_across, "sec", 2)
    second = make(0, quarter - lead, lead, f32)
    folded, second, beside = fence(folded, second, beside)
    second = second + beside[:, lead:].astype(f32)
    second_near = swap(second[rows:].astype(bf16), "dev", 1)
    first = make(0, lead, 0, f32)
    first, second_near, second_across = fence(first, second_near, second_across)
    first = first + beside[:, :lead].astype(f32) + first_across.astype(f32)
    first_near = swap(first[rows:].astype(bf16), "dev", 1)
    second = second[:rows] + second_near.astype(f32) + second_across.astype(f32)

    def halve(total, stride):
        count = total.shape[0] // 2
        sent = swap(total[count:].astype(bf16), "dev", stride)
        return total[:count] + sent.astype(f32)

    second = halve(second, strides[1])
    first_near, second = fence(first_near, second)
    first = halve(first[:rows] + first_near.astype(f32), strides[1])
    for stride in strides[2:]:
        second, first = halve(second, stride), halve(first, stride)
    return jnp.concatenate([first.astype(bf16), second.astype(bf16)], 1)


def solution(mesh):
    in_specs = (
        P("dev", "sec"),
        P("dev", None),
        P("dev", None),
        P(("sec", "dev"), None, None, None, None),
        P(("sec", "dev"), None, None, None),
        P(("sec", "dev"), None, None),
        P(("sec", "dev"), None),
        P(),
        P(),
    )
    out_specs = P("dev", "sec")
    return jax.shard_map(
        per_device, mesh=mesh, in_specs=in_specs, out_specs=out_specs, check_vma=False
    )
```

```python
import math

import jax
import jax.numpy as jnp
import numpy as np
from jax import lax
from jax.experimental import pallas as pl
from jax.experimental.pallas import tpu as pltpu
from jax.sharding import PartitionSpec as P

HAD = 128
LANES = 128
ROWS = 16
ROUTED_SCALE = 2.5
UNIT = 1.0 / math.sqrt(HAD)
f32, bf16, i16, i32 = jnp.float32, jnp.bfloat16, jnp.int16, jnp.int32


def hadamard_table(length):
    sylvester = np.ones((1, 1), np.float32)
    while sylvester.shape[0] < length:
        sylvester = np.concatenate(
            [np.concatenate([sylvester, sylvester], 1), np.concatenate([sylvester, -sylvester], 1)],
            0,
        )
    return sylvester


def coded_order(group):
    return np.arange(HAD).reshape(HAD // group, group).T.reshape(-1)


def dot(left, right):
    return jnp.dot(left, right, preferred_element_type=f32)


def lookup(table, index):
    dims = lax.GatherDimensionNumbers(
        offset_dims=(),
        collapsed_slice_dims=(1,),
        start_index_map=(1,),
        operand_batching_dims=(0,),
        start_indices_batching_dims=(0,),
    )
    return lax.gather(
        table, index[..., None], dims, (1, 1), mode=lax.GatherScatterMode.PROMISE_IN_BOUNDS
    )


def book_tables(books):
    lead = books.shape[:-2]
    entries, group = books.shape[-2:]
    halves = entries // LANES
    turned = jnp.swapaxes(books, -1, -2).reshape(lead + (group, halves, 1, LANES))
    return jnp.broadcast_to(turned, lead + (group, halves, ROWS, LANES))


def decode_tile(code_words, table, group):
    sums = [None] * group
    for book in range(2):
        words = code_words(book).astype(i16)
        low = words & (LANES - 1)
        upper = words > LANES - 1
        found = [
            (lookup(table(book, i, 0), low), lookup(table(book, i, 1), low)) for i in range(group)
        ]
        for i in range(group):
            value = jnp.where(upper, found[i][1], found[i][0])
            sums[i] = value if book == 0 else sums[i] + value
    return sums


def decode_in(section, codes, tables, weights, piece, cols, stored):
    _, mats, books, groups, hidden = codes.shape
    sections = stored + 1
    group = tables.shape[2]
    share = groups // sections
    per_mat = hidden // cols
    mat, block = piece // per_mat, piece % per_mat

    def body(section_ref, codes_ref, tables_ref, *rest):
        out = rest[-1]
        for h in range(cols // LANES):
            lanes = slice(h * LANES, (h + 1) * LANES)
            for g in range(share // ROWS):
                tiles = decode_tile(
                    lambda c: codes_ref[0, 0, c, g * ROWS : (g + 1) * ROWS, lanes],
                    lambda c, i, half: tables_ref[0, c, i, half],
                    group,
                )
                for i in range(group):
                    at = (g * group + i) * ROWS
                    out[0, at : at + ROWS, lanes] = tiles[i]

    def source(j, s):
        return (0, mat, 0, jnp.bitwise_xor(s[0], (j % 2) * 2 + j // 2), block)

    in_specs = [
        pl.BlockSpec((1, 1, books, share, cols), source),
        pl.BlockSpec((1,) + tables.shape[1:], lambda j, s: (mat, 0, 0, 0, 0, 0)),
    ]
    operands = [section, codes, tables]
    aliases = {}
    if weights is not None:
        in_specs.append(pl.BlockSpec(memory_space=pl.ANY))
        operands.append(weights)
        aliases = {3: 0}
    return pl.pallas_call(
        body,
        grid_spec=pltpu.PrefetchScalarGridSpec(
            num_scalar_prefetch=1,
            grid=(stored,),
            in_specs=in_specs,
            out_specs=pl.BlockSpec((1, share * group, cols), lambda j, s: (mat, j, block)),
        ),
        out_shape=jax.ShapeDtypeStruct((mats, stored * share * group, hidden), bf16),
        input_output_aliases=aliases,
        compiler_params=pltpu.CompilerParams(vmem_limit_bytes=50 << 20),
        name="decode_in",
    )(*operands)


def rotate(values, table):
    rows, blocks = values.shape[0], values.shape[1] // HAD
    tall = jnp.concatenate([values[:, b * HAD : (b + 1) * HAD] for b in range(blocks)], 0)
    tall = (dot(tall, table) * UNIT).astype(bf16)
    return jnp.concatenate([tall[b * rows : (b + 1) * rows] for b in range(blocks)], 1)


def project(section, codes, tables, weights, pick, pieces, signs, middle, had, order, places):
    _, mats, books, groups, hidden = codes.shape
    sections = len(places)
    group = tables.shape[2]
    share = groups // sections
    slots, token_total = pick.shape
    width = pieces[0].shape[1]
    chunks = len(pieces) // sections
    stored = weights.shape[1]
    cols = 512
    per_mat = hidden // cols
    pair = 2

    def body(*refs):
        section_ref, codes_ref, tables_ref, weights_ref, pick_ref = refs[:5]
        piece_refs = refs[5 : 5 + len(pieces)]
        signs_ref, middle_ref, had_ref, out, turned, total = refs[5 + len(pieces) :]
        step = pl.program_id(0) * per_mat + pl.program_id(1)

        @pl.when(step == 0)
        def _():
            for at, piece in enumerate(piece_refs):
                quarter = jnp.bitwise_xor(section_ref[0], places[at // chunks])
                start = pl.multiple_of((quarter * chunks + at % chunks) * width, LANES)
                front = (2 * signs_ref[0, 0:1, pl.ds(start, width)] - 1).astype(bf16)
                rows = dot(pick_ref[...], piece[...]).astype(bf16) * front
                turned[:, at * width : (at + 1) * width] = rotate(rows, had_ref[...])

        part = dot(turned[:, :stored], weights_ref[0])
        depth = pair * group * ROWS
        for p in range(share // ROWS // pair):
            strips = []
            for lane in range(0, cols, LANES):
                tiles = []
                for g in range(p * pair, (p + 1) * pair):
                    tiles += decode_tile(
                        lambda c: codes_ref[
                            0, 0, c, g * ROWS : (g + 1) * ROWS, lane : lane + LANES
                        ],
                        lambda c, i, half: tables_ref[0, c, i, half],
                        group,
                    )
                strips.append(jnp.concatenate(tiles, 0))
            at = stored + p * depth
            part = part + dot(turned[:, at : at + depth], jnp.concatenate(strips, 1))
        total[step] = part

        @pl.when(step == mats * per_mat - 1)
        def _():
            for h in range(per_mat):
                lanes = slice(h * cols, (h + 1) * cols)
                acted = (jax.nn.silu(total[h]) * total[per_mat + h]).astype(bf16)
                flips = (2 * middle_ref[:, lanes] - 1).astype(bf16)
                out[:, lanes] = rotate(acted * flips, had_ref[...])

    whole = lambda shape: pl.BlockSpec(shape, lambda m, h, s: (0,) * len(shape))
    return pl.pallas_call(
        body,
        grid_spec=pltpu.PrefetchScalarGridSpec(
            num_scalar_prefetch=1,
            grid=(mats, per_mat),
            in_specs=[
                pl.BlockSpec(
                    (1, 1, books, share, cols),
                    lambda m, h, s: (0, m, 0, jnp.bitwise_xor(s[0], order), h),
                ),
                pl.BlockSpec((1,) + tables.shape[1:], lambda m, h, s: (m, 0, 0, 0, 0, 0)),
                pl.BlockSpec((1, stored, cols), lambda m, h, s: (m, 0, h)),
                whole(pick.shape),
            ]
            + [whole(p.shape) for p in pieces]
            + [whole(signs.shape), whole(middle.shape), whole(had.shape)],
            out_specs=whole((slots, hidden)),
            scratch_shapes=[
                pltpu.VMEM((slots, groups * group), bf16),
                pltpu.VMEM((mats * per_mat, slots, cols), f32),
            ],
        ),
        out_shape=jax.ShapeDtypeStruct((slots, hidden), bf16),
        compiler_params=pltpu.CompilerParams(vmem_limit_bytes=50 << 20),
        name="project",
    )(section, codes, tables, weights, pick, *pieces, signs, middle, had)


def produce(section, codes, tables, folded, signs, had, spread, order, cols, at_col, dtype):
    _, books, groups, width = codes.shape
    sections = 4
    group = tables.shape[1]
    slots, hidden = folded.shape
    token_total = spread.shape[0]
    per_quarter = width // sections // cols
    tile = 2 * LANES
    pair = 2

    def body(section_ref, codes_ref, tables_ref, folded_ref, signs_ref, had_ref, spread_ref, out):
        back = (2 * signs_ref[0, 1:2, :] - 1).astype(f32)

        def outcome_of(at, size):
            outcome = None
            for p in range(groups // ROWS // pair):
                strips = []
                for lane in range(at, at + size, LANES):
                    tiles = []
                    for g in range(p * pair, (p + 1) * pair):
                        tiles += decode_tile(
                            lambda c: codes_ref[0, c, g * ROWS : (g + 1) * ROWS, lane : lane + LANES],
                            lambda c, i, half: tables_ref[c, i, half],
                            group,
                        )
                    strips.append(jnp.concatenate(tiles, 0))
                depth = pair * group * ROWS
                part = dot(folded_ref[:, p * depth : (p + 1) * depth], jnp.concatenate(strips, 1))
                outcome = part if outcome is None else outcome + part
            return outcome

        def finish(outcome, at, size):
            high = outcome.astype(bf16)
            left = outcome - high.astype(f32)
            mid = left.astype(bf16)
            low = (left - mid.astype(f32)).astype(bf16)
            table = had_ref[...]
            turned = []
            for b in range(0, size, HAD):
                s = slice(b, b + HAD)
                turned.append(dot(high[:, s], table) + (dot(mid[:, s], table) + dot(low[:, s], table)))
            turned = jnp.concatenate(turned, 1) * UNIT
            result = (back[:, at : at + size] * turned).astype(bf16)
            out[:, at : at + size] = dot(spread_ref[...], result).astype(dtype)

        pending = None
        at = 0
        while at < cols:
            size = min(tile, cols - at)
            outcome = outcome_of(at, size)
            if pending is not None:
                finish(*pending)
            pending = (outcome, at, size)
            at += size
        finish(*pending)

    def column(s):
        return jnp.bitwise_xor(s[0], order) * per_quarter + at_col

    whole = lambda shape: pl.BlockSpec(shape, lambda j, s: (0,) * len(shape))
    return pl.pallas_call(
        body,
        grid_spec=pltpu.PrefetchScalarGridSpec(
            num_scalar_prefetch=1,
            grid=(1,),
            in_specs=[
                pl.BlockSpec((1, books, groups, cols), lambda j, s: (0, 0, 0, column(s))),
                whole(tables.shape),
                whole(folded.shape),
                pl.BlockSpec((1, 2, cols), lambda j, s: (0, 0, column(s))),
                whole(had.shape),
                whole(spread.shape),
            ],
            out_specs=whole((token_total, cols)),
        ),
        out_shape=jax.ShapeDtypeStruct((token_total, cols), dtype),
        compiler_params=pltpu.CompilerParams(vmem_limit_bytes=20 << 20),
        name="produce",
    )(section, codes, tables, folded, signs, had, spread)


def swap(values, axis, stride):
    size = lax.axis_size(axis)
    return lax.ppermute(values, axis, [(i, i ^ stride) for i in range(size)])


def per_device(
    tokens,
    routes,
    scores,
    gate_up_codes,
    down_codes,
    model_signs,
    hidden_signs,
    gate_up_books,
    down_books,
):
    sections = lax.axis_size("sec")
    devices = lax.axis_size("dev")
    section = lax.axis_index("sec")
    device = lax.axis_index("dev")
    token_count, quarter = tokens.shape
    width = quarter * sections
    token_total = token_count * devices
    slots = 4 * token_count
    group = gate_up_books.shape[-1]
    chunks = 2
    half = quarter // chunks
    strides = [1 << b for b in range(devices.bit_length() - 1)]
    section_word = section.astype(i32).reshape(1)

    relative = [0]
    for stride in reversed(strides):
        relative = relative + [b ^ stride for b in relative]
    places = [0, 2, 1, 3]

    gates = (ROUTED_SCALE * scores / jnp.sum(scores, axis=1, keepdims=True)).astype(bf16)
    top = routes.shape[1]
    tables_in = book_tables(gate_up_books)
    tables_down = book_tables(down_books)
    sylvester = hadamard_table(HAD)
    had_coded = jnp.asarray(sylvester[:, coded_order(group)], bf16)
    had = jnp.asarray(sylvester, bf16)

    def fence(*values):
        return lax.optimization_barrier(values)

    facts = jnp.concatenate([routes.astype(bf16), gates], 1)
    facts = jnp.pad(facts, ((0, 0), (0, LANES - 2 * top)))
    row = jnp.concatenate([tokens, facts], 1)
    gathered = [row] + [swap(row, "dev", b) for b in relative[1 : devices // 2]]

    def piece_of(stack, piece):
        return decode_in(
            section_word, gate_up_codes, tables_in, stack, piece, hidden // 2, sections - 1
        )

    hidden = gate_up_codes.shape[-1]
    weights = piece_of(None, 0)
    weights, gathered = fence(weights, gathered)
    gathered = jnp.concatenate(gathered, 0)
    first = jnp.concatenate([gathered[:, :half], gathered[:, quarter:]], 1)
    second = gathered[:, half:quarter]
    weights, first, second = fence(weights, first, second)
    first_near = swap(first, "dev", 1)
    second_cross = swap(second, "sec", 2)
    weights = piece_of(weights, 1)
    weights, first_near, second_cross = fence(weights, first_near, second_cross)
    first = jnp.concatenate([first, first_near], 0)
    first, facts = first[:, :half], first[:, half:].astype(f32)
    first_cross = swap(first, "sec", 2)
    second_near = swap(second, "dev", 1)
    second_both = swap(second_cross, "dev", 1)
    weights = piece_of(weights, 2)
    weights, first_cross, second_near, second_both = fence(
        weights, first_cross, second_near, second_both
    )
    second = jnp.concatenate([second, second_near], 0)
    second_cross = jnp.concatenate([second_cross, second_both], 0)
    pieces = [first, second, first_cross, second_cross]
    pieces = pieces + [swap(p, "sec", 1) for p in pieces]
    weights = piece_of(weights, 3)

    expert = ((section - 1) * devices + device).astype(f32)
    named = facts[:, :top] == expert
    hit = jnp.any(named, axis=1)
    gate = jnp.sum(jnp.where(named, facts[:, top : 2 * top], 0.0), axis=1)
    earlier = (jnp.arange(token_total)[:, None] < jnp.arange(token_total)[None, :]).astype(f32)
    slot = jnp.sum(jnp.where(hit[:, None], earlier, 0.0), axis=0)
    slot = jnp.where(hit, slot, -1.0)
    shared = section == 0
    token_id = jnp.arange(token_total)
    own = token_id < token_count
    slot = jnp.where(shared, jnp.where(own, token_id.astype(f32), -1.0), slot)
    gate = jnp.where(shared, 1.0, gate)
    slot_id = jnp.arange(slots).astype(f32)
    pick = (slot_id[:, None] == slot[None, :]).astype(bf16)
    spread = jnp.where(slot[:, None] == slot_id[None, :], gate[:, None], 0.0).astype(bf16)


    folded = project(
        section_word,
        gate_up_codes,
        tables_in,
        weights,
        pick,
        pieces,
        model_signs,
        hidden_signs,
        had_coded,
        places[3],
        places,
    )

    def make(order, cols=quarter, at_col=0, dtype=bf16):
        return produce(
            section_word,
            down_codes,
            tables_down,
            folded,
            model_signs,
            had,
            spread,
            order,
            cols,
            at_col,
            dtype,
        )

    rows = token_total // 2
    given = make(3)
    folded, given = fence(folded, given)
    given = swap(given, "sec", 1)
    across = make(2)
    folded, across, given = fence(folded, across, given)
    across = across.astype(f32) + given.astype(f32)
    early = half // LANES // 2 * LANES
    first_across = [across[:, :early].astype(bf16), across[:, early:half].astype(bf16)]
    second_met = across[rows:, half:].astype(bf16)
    second_kept = across[:rows, half:].astype(bf16)
    folded, *first_across, second_met, second_kept = fence(
        folded, *first_across, second_met, second_kept
    )
    first_across = [swap(f, "sec", 2) for f in first_across]
    second_met = swap(second_met, "dev", 1)
    beside = make(1)
    folded, beside, second_met, first_across[0] = fence(
        folded, beside, second_met, first_across[0]
    )
    beside = swap(beside, "sec", 1)
    second_across = (second_kept.astype(f32) + second_met.astype(f32)).astype(bf16)
    second_across = swap(second_across, "sec", 2)
    second = make(0, half, 1, f32)
    folded, second, beside = fence(folded, second, beside)
    second = second + beside[:, half:].astype(f32)
    second_near = swap(second[rows:].astype(bf16), "dev", 1)
    first = make(0, half, 0, f32)
    first, second_near = fence(first, second_near)
    first_across = jnp.concatenate(first_across, 1)
    first = first + beside[:, :half].astype(f32) + first_across.astype(f32)
    first_near = swap(first[rows:].astype(bf16), "dev", 1)
    second = second[:rows] + second_near.astype(f32) + second_across.astype(f32)
    first = first[:rows] + first_near.astype(f32)

    def collect(total):
        result = total[:token_count]
        for at in range(1, devices // 2):
            block = total[at * token_count : (at + 1) * token_count].astype(bf16)
            result = result + swap(block, "dev", relative[at]).astype(f32)
        return result.astype(bf16)

    second = collect(second)
    return jnp.concatenate([collect(first), second], 1)


def solution(mesh):
    in_specs = (
        P("dev", "sec"),
        P("dev", None),
        P("dev", None),
        P(("sec", "dev"), None, None, None, None),
        P(("sec", "dev"), None, None, None),
        P(("sec", "dev"), None, None),
        P(("sec", "dev"), None),
        P(),
        P(),
    )
    out_specs = P("dev", "sec")
    return jax.shard_map(
        per_device, mesh=mesh, in_specs=in_specs, out_specs=out_specs, check_vma=False
    )
```

```python
import math

import jax
import jax.numpy as jnp
import numpy as np
from jax import lax
from jax.experimental import pallas as pl
from jax.experimental.pallas import tpu as pltpu
from jax.sharding import PartitionSpec as P

HAD = 128
LANES = 128
ROWS = 16
ROUTED_SCALE = 2.5
UNIT = 1.0 / math.sqrt(HAD)
f32, bf16, i16, i32 = jnp.float32, jnp.bfloat16, jnp.int16, jnp.int32


def hadamard_table(length):
    sylvester = np.ones((1, 1), np.float32)
    while sylvester.shape[0] < length:
        sylvester = np.concatenate(
            [np.concatenate([sylvester, sylvester], 1), np.concatenate([sylvester, -sylvester], 1)],
            0,
        )
    return sylvester


def coded_order(group):
    return np.arange(HAD).reshape(HAD // group, group).T.reshape(-1)


def dot(left, right):
    return jnp.dot(left, right, preferred_element_type=f32)


def lookup(table, index):
    dims = lax.GatherDimensionNumbers(
        offset_dims=(),
        collapsed_slice_dims=(1,),
        start_index_map=(1,),
        operand_batching_dims=(0,),
        start_indices_batching_dims=(0,),
    )
    return lax.gather(
        table, index[..., None], dims, (1, 1), mode=lax.GatherScatterMode.PROMISE_IN_BOUNDS
    )


def book_tables(books):
    lead = books.shape[:-2]
    entries, group = books.shape[-2:]
    halves = entries // LANES
    turned = jnp.swapaxes(books, -1, -2).reshape(lead + (group, halves, 1, LANES))
    return jnp.broadcast_to(turned, lead + (group, halves, ROWS, LANES))


def decode_tile(code_words, table, group):
    sums = [None] * group
    for book in range(2):
        words = code_words(book).astype(i16)
        low = words & (LANES - 1)
        upper = words > LANES - 1
        found = [
            (lookup(table(book, i, 0), low), lookup(table(book, i, 1), low)) for i in range(group)
        ]
        for i in range(group):
            value = jnp.where(upper, found[i][1], found[i][0])
            sums[i] = value if book == 0 else sums[i] + value
    return sums


def decode_in(section, codes, tables, weights, piece, cols, stored):
    _, mats, books, groups, hidden = codes.shape
    sections = stored + 1
    group = tables.shape[2]
    share = groups // sections
    per_mat = hidden // cols
    mat, block = piece // per_mat, piece % per_mat

    def body(section_ref, codes_ref, tables_ref, *rest):
        out = rest[-1]
        for h in range(cols // LANES):
            lanes = slice(h * LANES, (h + 1) * LANES)
            for g in range(share // ROWS):
                tiles = decode_tile(
                    lambda c: codes_ref[0, 0, c, g * ROWS : (g + 1) * ROWS, lanes],
                    lambda c, i, half: tables_ref[0, c, i, half],
                    group,
                )
                for i in range(group):
                    at = (g * group + i) * ROWS
                    out[0, at : at + ROWS, lanes] = tiles[i]

    def source(j, s):
        return (0, mat, 0, jnp.bitwise_xor(s[0], (j % 2) * 2 + j // 2), block)

    in_specs = [
        pl.BlockSpec((1, 1, books, share, cols), source),
        pl.BlockSpec((1,) + tables.shape[1:], lambda j, s: (mat, 0, 0, 0, 0, 0)),
    ]
    operands = [section, codes, tables]
    aliases = {}
    if weights is not None:
        in_specs.append(pl.BlockSpec(memory_space=pl.ANY))
        operands.append(weights)
        aliases = {3: 0}
    return pl.pallas_call(
        body,
        grid_spec=pltpu.PrefetchScalarGridSpec(
            num_scalar_prefetch=1,
            grid=(stored,),
            in_specs=in_specs,
            out_specs=pl.BlockSpec((1, share * group, cols), lambda j, s: (mat, j, block)),
        ),
        out_shape=jax.ShapeDtypeStruct((mats, stored * share * group, hidden), bf16),
        input_output_aliases=aliases,
        compiler_params=pltpu.CompilerParams(vmem_limit_bytes=50 << 20),
        name="decode_in",
    )(*operands)


def rotate(values, table):
    rows, blocks = values.shape[0], values.shape[1] // HAD
    tall = jnp.concatenate([values[:, b * HAD : (b + 1) * HAD] for b in range(blocks)], 0)
    tall = (dot(tall, table) * UNIT).astype(bf16)
    return jnp.concatenate([tall[b * rows : (b + 1) * rows] for b in range(blocks)], 1)


def project(section, codes, tables, weights, pick, pieces, signs, middle, had, order, places):
    _, mats, books, groups, hidden = codes.shape
    sections = len(places)
    group = tables.shape[2]
    share = groups // sections
    slots, token_total = pick.shape
    width = pieces[0].shape[1]
    chunks = len(pieces) // sections
    stored = weights.shape[1]
    cols = 512
    per_mat = hidden // cols
    pair = 2

    def body(*refs):
        section_ref, codes_ref, tables_ref, weights_ref, pick_ref = refs[:5]
        piece_refs = refs[5 : 5 + len(pieces)]
        signs_ref, middle_ref, had_ref, out, turned, total = refs[5 + len(pieces) :]
        step = pl.program_id(0) * per_mat + pl.program_id(1)

        @pl.when(step == 0)
        def _():
            for at, piece in enumerate(piece_refs):
                quarter = jnp.bitwise_xor(section_ref[0], places[at // chunks])
                start = pl.multiple_of((quarter * chunks + at % chunks) * width, LANES)
                front = (2 * signs_ref[0, 0:1, pl.ds(start, width)] - 1).astype(bf16)
                rows = dot(pick_ref[...], piece[...]).astype(bf16) * front
                turned[:, at * width : (at + 1) * width] = rotate(rows, had_ref[...])

        part = dot(turned[:, :stored], weights_ref[0])
        depth = pair * group * ROWS
        for p in range(share // ROWS // pair):
            strips = []
            for lane in range(0, cols, LANES):
                tiles = []
                for g in range(p * pair, (p + 1) * pair):
                    tiles += decode_tile(
                        lambda c: codes_ref[
                            0, 0, c, g * ROWS : (g + 1) * ROWS, lane : lane + LANES
                        ],
                        lambda c, i, half: tables_ref[0, c, i, half],
                        group,
                    )
                strips.append(jnp.concatenate(tiles, 0))
            at = stored + p * depth
            part = part + dot(turned[:, at : at + depth], jnp.concatenate(strips, 1))
        total[step] = part

        @pl.when(step == mats * per_mat - 1)
        def _():
            for h in range(per_mat):
                lanes = slice(h * cols, (h + 1) * cols)
                acted = (jax.nn.silu(total[h]) * total[per_mat + h]).astype(bf16)
                flips = (2 * middle_ref[:, lanes] - 1).astype(bf16)
                out[:, lanes] = rotate(acted * flips, had_ref[...])

    whole = lambda shape: pl.BlockSpec(shape, lambda m, h, s: (0,) * len(shape))
    return pl.pallas_call(
        body,
        grid_spec=pltpu.PrefetchScalarGridSpec(
            num_scalar_prefetch=1,
            grid=(mats, per_mat),
            in_specs=[
                pl.BlockSpec(
                    (1, 1, books, share, cols),
                    lambda m, h, s: (0, m, 0, jnp.bitwise_xor(s[0], order), h),
                ),
                pl.BlockSpec((1,) + tables.shape[1:], lambda m, h, s: (m, 0, 0, 0, 0, 0)),
                pl.BlockSpec((1, stored, cols), lambda m, h, s: (m, 0, h)),
                whole(pick.shape),
            ]
            + [whole(p.shape) for p in pieces]
            + [whole(signs.shape), whole(middle.shape), whole(had.shape)],
            out_specs=whole((slots, hidden)),
            scratch_shapes=[
                pltpu.VMEM((slots, groups * group), bf16),
                pltpu.VMEM((mats * per_mat, slots, cols), f32),
            ],
        ),
        out_shape=jax.ShapeDtypeStruct((slots, hidden), bf16),
        compiler_params=pltpu.CompilerParams(vmem_limit_bytes=50 << 20),
        name="project",
    )(section, codes, tables, weights, pick, *pieces, signs, middle, had)


def produce(section, codes, tables, folded, signs, had, spread, order, cols, at_col, dtype):
    _, books, groups, width = codes.shape
    sections = 4
    group = tables.shape[1]
    slots, hidden = folded.shape
    token_total = spread.shape[0]
    per_quarter = width // sections // cols
    tile = 2 * LANES
    pair = 2

    def body(section_ref, codes_ref, tables_ref, folded_ref, signs_ref, had_ref, spread_ref, out):
        back = (2 * signs_ref[0, 1:2, :] - 1).astype(f32)

        def outcome_of(at, size):
            outcome = None
            for p in range(groups // ROWS // pair):
                strips = []
                for lane in range(at, at + size, LANES):
                    tiles = []
                    for g in range(p * pair, (p + 1) * pair):
                        tiles += decode_tile(
                            lambda c: codes_ref[0, c, g * ROWS : (g + 1) * ROWS, lane : lane + LANES],
                            lambda c, i, half: tables_ref[c, i, half],
                            group,
                        )
                    strips.append(jnp.concatenate(tiles, 0))
                depth = pair * group * ROWS
                part = dot(folded_ref[:, p * depth : (p + 1) * depth], jnp.concatenate(strips, 1))
                outcome = part if outcome is None else outcome + part
            return outcome

        def finish(outcome, at, size):
            high = outcome.astype(bf16)
            left = outcome - high.astype(f32)
            mid = left.astype(bf16)
            low = (left - mid.astype(f32)).astype(bf16)
            table = had_ref[...]
            cuts = [slice(b, b + HAD) for b in range(0, size, HAD)]
            tall = jnp.concatenate([part[:, cut] for part in (high, mid, low) for cut in cuts], 0)
            tall = dot(tall, table)
            count = len(cuts)
            parts = [tall[b * slots : (b + 1) * slots] for b in range(3 * count)]
            turned = [
                parts[b] + (parts[count + b] + parts[2 * count + b]) for b in range(count)
            ]
            turned = jnp.concatenate(turned, 1) * UNIT
            result = (back[:, at : at + size] * turned).astype(bf16)
            out[:, at : at + size] = dot(spread_ref[...], result).astype(dtype)

        pending = None
        at = 0
        while at < cols:
            size = min(tile, cols - at)
            outcome = outcome_of(at, size)
            if pending is not None:
                finish(*pending)
            pending = (outcome, at, size)
            at += size
        finish(*pending)

    def column(s):
        return jnp.bitwise_xor(s[0], order) * per_quarter + at_col

    whole = lambda shape: pl.BlockSpec(shape, lambda j, s: (0,) * len(shape))
    return pl.pallas_call(
        body,
        grid_spec=pltpu.PrefetchScalarGridSpec(
            num_scalar_prefetch=1,
            grid=(1,),
            in_specs=[
                pl.BlockSpec((1, books, groups, cols), lambda j, s: (0, 0, 0, column(s))),
                whole(tables.shape),
                whole(folded.shape),
                pl.BlockSpec((1, 2, cols), lambda j, s: (0, 0, column(s))),
                whole(had.shape),
                whole(spread.shape),
            ],
            out_specs=whole((token_total, cols)),
        ),
        out_shape=jax.ShapeDtypeStruct((token_total, cols), dtype),
        compiler_params=pltpu.CompilerParams(vmem_limit_bytes=20 << 20),
        name="produce",
    )(section, codes, tables, folded, signs, had, spread)


def swap(values, axis, stride):
    size = lax.axis_size(axis)
    return lax.ppermute(values, axis, [(i, i ^ stride) for i in range(size)])


def per_device(
    tokens,
    routes,
    scores,
    gate_up_codes,
    down_codes,
    model_signs,
    hidden_signs,
    gate_up_books,
    down_books,
):
    sections = lax.axis_size("sec")
    devices = lax.axis_size("dev")
    section = lax.axis_index("sec")
    device = lax.axis_index("dev")
    token_count, quarter = tokens.shape
    width = quarter * sections
    token_total = token_count * devices
    slots = 4 * token_count
    group = gate_up_books.shape[-1]
    chunks = 2
    half = quarter // chunks
    strides = [1 << b for b in range(devices.bit_length() - 1)]
    section_word = section.astype(i32).reshape(1)

    relative = [0]
    for stride in reversed(strides):
        relative = relative + [b ^ stride for b in relative]
    places = [0, 2, 1, 3]

    gates = (ROUTED_SCALE * scores / jnp.sum(scores, axis=1, keepdims=True)).astype(bf16)
    top = routes.shape[1]
    tables_in = book_tables(gate_up_books)
    tables_down = book_tables(down_books)
    sylvester = hadamard_table(HAD)
    had_coded = jnp.asarray(sylvester[:, coded_order(group)], bf16)
    had = jnp.asarray(sylvester, bf16)

    def fence(*values):
        return lax.optimization_barrier(values)

    facts = jnp.concatenate([routes.astype(bf16), gates], 1)
    facts = jnp.pad(facts, ((0, 0), (0, LANES - 2 * top)))
    row = jnp.concatenate([tokens, facts], 1)
    gathered = [row] + [swap(row, "dev", b) for b in relative[1 : devices // 2]]

    def piece_of(stack, piece):
        return decode_in(
            section_word, gate_up_codes, tables_in, stack, piece, hidden // 2, sections - 1
        )

    hidden = gate_up_codes.shape[-1]
    weights = piece_of(None, 0)
    weights, gathered = fence(weights, gathered)
    gathered = jnp.concatenate(gathered, 0)
    first = jnp.concatenate([gathered[:, :half], gathered[:, quarter:]], 1)
    second = gathered[:, half:quarter]
    weights, first, second = fence(weights, first, second)
    first_near = swap(first, "dev", 1)
    second_cross = swap(second, "sec", 2)
    weights = piece_of(weights, 1)
    weights, first_near, second_cross = fence(weights, first_near, second_cross)
    first = jnp.concatenate([first, first_near], 0)
    first, facts = first[:, :half], first[:, half:].astype(f32)
    first_cross = swap(first, "sec", 2)
    second_near = swap(second, "dev", 1)
    second_both = swap(second_cross, "dev", 1)
    weights = piece_of(weights, 2)
    weights, first_cross, second_near, second_both = fence(
        weights, first_cross, second_near, second_both
    )
    second = jnp.concatenate([second, second_near], 0)
    second_cross = jnp.concatenate([second_cross, second_both], 0)
    pieces = [first, second, first_cross, second_cross]
    pieces = pieces + [swap(p, "sec", 1) for p in pieces]
    weights = piece_of(weights, 3)

    expert = ((section - 1) * devices + device).astype(f32)
    named = facts[:, :top] == expert
    hit = jnp.any(named, axis=1)
    gate = jnp.sum(jnp.where(named, facts[:, top : 2 * top], 0.0), axis=1)
    earlier = (jnp.arange(token_total)[:, None] < jnp.arange(token_total)[None, :]).astype(f32)
    slot = jnp.sum(jnp.where(hit[:, None], earlier, 0.0), axis=0)
    slot = jnp.where(hit, slot, -1.0)
    shared = section == 0
    token_id = jnp.arange(token_total)
    own = token_id < token_count
    slot = jnp.where(shared, jnp.where(own, token_id.astype(f32), -1.0), slot)
    gate = jnp.where(shared, 1.0, gate)
    slot_id = jnp.arange(slots).astype(f32)
    pick = (slot_id[:, None] == slot[None, :]).astype(bf16)
    spread = jnp.where(slot[:, None] == slot_id[None, :], gate[:, None], 0.0).astype(bf16)


    folded = project(
        section_word,
        gate_up_codes,
        tables_in,
        weights,
        pick,
        pieces,
        model_signs,
        hidden_signs,
        had_coded,
        places[3],
        places,
    )

    def make(order, cols=quarter, at_col=0, dtype=bf16):
        return produce(
            section_word,
            down_codes,
            tables_down,
            folded,
            model_signs,
            had,
            spread,
            order,
            cols,
            at_col,
            dtype,
        )

    rows = token_total // 2
    given = make(3)
    folded, given = fence(folded, given)
    given = swap(given, "sec", 1)
    across = make(2)
    folded, across, given = fence(folded, across, given)
    across = across.astype(f32) + given.astype(f32)
    early = half // LANES // 2 * LANES
    first_across = [across[:, :early].astype(bf16), across[:, early:half].astype(bf16)]
    second_met = across[rows:, half:].astype(bf16)
    second_kept = across[:rows, half:].astype(bf16)
    folded, *first_across, second_met, second_kept = fence(
        folded, *first_across, second_met, second_kept
    )
    first_across = [swap(f, "sec", 2) for f in first_across]
    second_met = swap(second_met, "dev", 1)
    beside = make(1)
    folded, beside, second_met, first_across[0] = fence(
        folded, beside, second_met, first_across[0]
    )
    beside = swap(beside, "sec", 1)
    second_across = (second_kept.astype(f32) + second_met.astype(f32)).astype(bf16)
    second_across = swap(second_across, "sec", 2)
    second = make(0, half, 1, f32)
    folded, second, beside = fence(folded, second, beside)
    second = second + beside[:, half:].astype(f32)
    second_near = swap(second[rows:].astype(bf16), "dev", 1)
    first = make(0, half, 0, f32)
    first, second_near = fence(first, second_near)
    first_across = jnp.concatenate(first_across, 1)
    first = first + beside[:, :half].astype(f32) + first_across.astype(f32)
    first_near = swap(first[rows:].astype(bf16), "dev", 1)
    second = second[:rows] + second_near.astype(f32) + second_across.astype(f32)
    first = first[:rows] + first_near.astype(f32)

    def collect(total):
        result = total[:token_count]
        for at in range(1, devices // 2):
            block = total[at * token_count : (at + 1) * token_count].astype(bf16)
            result = result + swap(block, "dev", relative[at]).astype(f32)
        return result.astype(bf16)

    second = collect(second)
    return jnp.concatenate([collect(first), second], 1)


def solution(mesh):
    in_specs = (
        P("dev", "sec"),
        P("dev", None),
        P("dev", None),
        P(("sec", "dev"), None, None, None, None),
        P(("sec", "dev"), None, None, None),
        P(("sec", "dev"), None, None),
        P(("sec", "dev"), None),
        P(),
        P(),
    )
    out_specs = P("dev", "sec")
    return jax.shard_map(
        per_device, mesh=mesh, in_specs=in_specs, out_specs=out_specs, check_vma=False
    )
```
